32 devices in a mesh: grp: 4 (over y, core), idx: 8 (over z, x).
Axes of the slice: x: 2, y: 2, z: 4, core: 2. Of those that a mesh axis runs over, the one named last changes fastest.
Arguments:
- queries: bfloat16 [8, 1024, 768], P('idx', 'grp'), may hold values from -6 to 6
- passages: bfloat16 [8, 1024, 768], P('idx', 'grp'), may hold values from -6 to 6
- partner: int32 [2, 8], replicated, may hold values from 0 to 7, each once within a row
- pair_codes: int32 [2, 8, 4, 16], P(None, None, 'grp'), may hold values from 0 to 15, as said below
- pair_count: int32 [2, 8, 4], P(None, None, 'grp'), may hold values from 4 to 16, as said below
- positive: int32 [8, 1024], P('idx', 'grp'), may hold values from 0 to 1023
Outputs:
- query_grad: float32 [8, 1024, 768], P('idx', 'grp')
- passage_grad: float32 [8, 1024, 768], P('idx', 'grp')
The draws below stay inside these ranges and needn't reach their ends.
Inputs may be any that keep to these rules, and one draw needn't show every extreme that they name: Each row of partner is a permutation of the clusters: in round r the queries of cluster c are scored against the panel of cluster partner[r, c]. `pair_codes`: the 16 codes of one list are distinct. `pair_count`: in every round at least one list has all 16 slots live.
All inputs are finite; a program needn't handle non-finite values.
Results may differ from the reference program's by a relative error of at most 0.0034.
Values may be sent and summed in bfloat16 or wider, within the bound.
A program may use at most 128 MiB of HBM per device.

```python
import jax
import jax.numpy as jnp
from jax import lax

D = 768
BLK = 128
ROUNDS = 2
PDEV = 256
NBLK = 16
NCL = 8
QSET = 1024
PROWS = 1024
QB = 8
PB = 2
N_GRP = 4
N_IDX = 8


def draw_pair_codes(key, part):
    key_list = jax.random.split(key, ROUNDS * N_IDX * N_GRP)

    def one_list(list_key):
        return jax.random.permutation(list_key, QB * PB)[:NBLK]
    drawn = jax.vmap(one_list)(key_list)
    return drawn.reshape(ROUNDS, N_IDX, N_GRP, NBLK).astype(jnp.int32)


def draw_pair_count(key, part):
    base_key = jax.random.fold_in(key, 11)
    pick_key = jax.random.fold_in(key, 23)
    base_counts = jax.random.randint(base_key, (ROUNDS, N_IDX, N_GRP), max(1, NBLK // 4), NBLK + 1)
    chosen = jax.random.randint(pick_key, (ROUNDS, 1, 1), 0, N_IDX * N_GRP)
    flat_index = (jnp.arange(N_IDX, dtype=jnp.int32)[:, None] * N_GRP + jnp.arange(N_GRP, dtype=jnp.int32)[None, :])[None]
    return jnp.where(flat_index == chosen, NBLK, base_counts).astype(jnp.int32)


def with_ends(entries, rng, smallest, largest):
    extent = entries.shape
    spot = [jax.random.randint(jax.random.fold_in(rng, axis), (), 0, extent[axis]) for axis in range(len(extent))]
    entries = entries.at[tuple(spot)].set(smallest)
    longest = extent.index(max(extent))
    spot[longest] = (spot[longest] + 1) % extent[longest]
    return entries.at[tuple(spot)].set(largest)


def block_levels(stream_key, shape, pieces, smallest, largest):
    loudness = 1.0
    for dim, shards_of in pieces:
        draws = jax.random.uniform(jax.random.fold_in(jax.random.fold_in(stream_key, 6), dim), (shards_of,), jnp.float32, smallest / len(pieces), largest / len(pieces))
        loudness = loudness * jnp.repeat(jnp.exp(draws), shape[dim] // shards_of).reshape((-1,) + (1,) * (len(shape) - 1 - dim))
    return loudness


def bell_draw(stream_key, dims, deviation, most, shards=(), kind=jnp.bfloat16):
    result = jax.random.normal(stream_key, dims, jnp.float32) * deviation
    if len(shards) > 0:
        result = block_levels(stream_key, dims, shards, -0.22, 0.18) * result
    return jnp.clip(result, min=-most, max=most).astype(kind)


def setup_inputs(seed: int = 0) -> dict:
    seeds = jax.random.split(jax.random.key(seed), 7)
    return {
        "queries": bell_draw(seeds[0], (NCL, QSET, D), 1.0, 6.0, ((0, 8), (1, 4))),
        "passages": bell_draw(seeds[1], (NCL, PROWS, D), 1.0, 6.0, ((0, 8), (1, 4))),
        "partner": jax.vmap(lambda own: jax.random.permutation(own, NCL))(jax.random.split(seeds[2], ROUNDS)).reshape((ROUNDS, NCL)).astype(jnp.int32),
        "pair_codes": draw_pair_codes(jax.random.fold_in(seeds[6], 71), 0),
        "pair_count": draw_pair_count(jax.random.fold_in(seeds[6], 71), 0),
        "positive": with_ends(jax.random.randint(seeds[5], (NCL, QSET), 0, PROWS), jax.random.fold_in(seeds[5], 1), 0, PROWS - 1).astype(jnp.int32),
    }


positive_weight = 16.0


def score_list(query_set, panel_shard, pair_list, live_count, logit_scale):
    query_tiles = query_set.shape[0] // BLK
    panel_tiles = panel_shard.shape[0] // BLK
    columns = query_set.shape[1]
    query_index = pair_list // panel_tiles
    panel_index = pair_list % panel_tiles
    slot_total = pair_list.shape[0]
    live_mask = (jnp.arange(slot_total, dtype=jnp.int32) < live_count).astype(jnp.float32)
    query_block_list = jnp.take(query_set.reshape(query_tiles, BLK, columns), query_index, axis=0).astype(jnp.float32)
    panel_block_list = jnp.take(panel_shard.reshape(panel_tiles, BLK, columns), panel_index, axis=0).astype(jnp.float32)
    similarity_scores = logit_scale * jnp.einsum("wzr,wlr->wzl", query_block_list, panel_block_list)
    sample_weights = (jax.nn.sigmoid(similarity_scores) * live_mask[:, None, None]).astype(jnp.bfloat16)
    sample_weights = lax.optimization_barrier(sample_weights).astype(jnp.float32)
    query_portion = jnp.einsum("nku,nua->nka", sample_weights, panel_block_list)
    panel_portion = jnp.einsum("swc,swj->scj", sample_weights, query_block_list)
    query_sum = jax.ops.segment_sum(query_portion, query_index, num_segments=query_tiles)
    panel_sum = jax.ops.segment_sum(panel_portion, panel_index, num_segments=panel_tiles)
    return logit_scale * query_sum.reshape(query_set.shape), logit_scale * panel_sum.reshape(panel_shard.shape)


def positive_terms(query_set, panel, targets, logit_scale):
    target_rows = jnp.take(panel, targets, axis=0).astype(jnp.float32)
    similarity_scores = logit_scale * jnp.sum(query_set.astype(jnp.float32) * target_rows, axis=1)
    factor = positive_weight * (jax.nn.sigmoid(similarity_scores) - 1.0)
    query_near = logit_scale * factor[:, None] * target_rows
    panel_near = logit_scale * jax.ops.segment_sum(factor[:, None] * query_set.astype(jnp.float32), targets, num_segments=panel.shape[0])
    return query_near, panel_near


def reference(queries, passages, partner, pair_codes, pair_count, positive):
    logit_scale = D ** -0.5
    inverse = jnp.argsort(partner, axis=1).astype(jnp.int32)
    clusters = jnp.arange(NCL, dtype=jnp.int32)

    def near_cluster(cluster):
        return positive_terms(queries[cluster], passages[cluster], positive[cluster], logit_scale)

    query_total, passage_total = lax.map(near_cluster, clusters)
    for pass_index in range(ROUNDS):
        def far_cluster(cluster):
            source_panel = passages[partner[pass_index, cluster]]
            query_set = queries[cluster]
            query_sum = jnp.zeros((QSET, D), jnp.float32)
            shard_grads = []
            for member in range(N_GRP):
                shard = lax.dynamic_slice_in_dim(source_panel, member * PDEV, PDEV, 0)
                query_portion, panel_portion = score_list(query_set, shard, pair_codes[pass_index, cluster, member], pair_count[pass_index, cluster, member], logit_scale)
                query_sum = query_sum + query_portion
                shard_grads.append(panel_portion.astype(jnp.bfloat16))
            return query_sum, jnp.concatenate(shard_grads, axis=0)

        query_far, passage_far = lax.map(far_cluster, clusters)
        passage_far = lax.optimization_barrier(passage_far)
        query_total = query_total + query_far
        passage_total = passage_total + jnp.take(passage_far, inverse[pass_index], axis=0).astype(jnp.float32)
    return query_total, passage_total
```

```python
import functools
import math

import jax
import jax.numpy as jnp
from jax import lax
from jax.experimental import pallas as pl
from jax.experimental.pallas import tpu as pltpu
from jax.sharding import PartitionSpec as P

BLK = 128


positive_weight = 16.0


def score_list(query_set, panel_shard, pair_list, live_count, logit_scale):
    query_tiles = query_set.shape[0] // BLK
    panel_tiles = panel_shard.shape[0] // BLK
    columns = query_set.shape[1]
    slot_total = pair_list.shape[0]
    group_size = math.gcd(48, slot_total)
    query_grid = query_set.reshape(query_tiles, BLK, columns)
    panel_grid = panel_shard.reshape(panel_tiles, BLK, columns)

    def one_group(turn_index, partial_sums):
        query_acc, panel_acc = partial_sums
        first_slot = turn_index * group_size
        live_mask = first_slot + jnp.arange(group_size, dtype=jnp.int32) < live_count
        query_index = pair_list // panel_tiles
        panel_index = pair_list % panel_tiles
        query_block_list = jnp.take(query_grid, query_index, axis=0)
        panel_block_list = jnp.take(panel_grid, panel_index, axis=0)
        similarity_scores = logit_scale * jnp.einsum(
            "wzr,wlr->wzl", query_block_list, panel_block_list, preferred_element_type=jnp.float32
        )
        sample_weights = jnp.where(
            live_mask[:, None, None], jax.nn.sigmoid(similarity_scores), 0.0
        ).astype(jnp.bfloat16)
        query_portion = jnp.einsum(
            "nku,nua->nka", sample_weights, panel_block_list, preferred_element_type=jnp.float32
        )
        panel_portion = jnp.einsum(
            "swc,swj->scj", sample_weights, query_block_list, preferred_element_type=jnp.float32
        )
        query_acc = query_acc + jax.ops.segment_sum(
            query_portion, query_index, num_segments=query_tiles
        )
        panel_acc = panel_acc + jax.ops.segment_sum(
            panel_portion, panel_index, num_segments=panel_tiles
        )
        return (query_acc, panel_acc)

    start_sums = (
        jnp.zeros(query_grid.shape, jnp.float32),
        jnp.zeros(panel_grid.shape, jnp.float32),
    )
    turn_total = slot_total // group_size
    query_acc, panel_acc = lax.fori_loop(0, turn_total, one_group, start_sums)
    return (
        logit_scale * query_acc.reshape(query_set.shape),
        logit_scale * panel_acc.reshape(panel_shard.shape),
    )


def near_terms(query_set, targets, own_panel, row_offset, logit_scale):
    row_total = own_panel.shape[0]
    local_rows = targets - row_offset
    owned = (local_rows >= 0) & (local_rows < row_total)
    safe_rows = jnp.clip(local_rows, 0, row_total - 1)
    target_rows = jnp.take(own_panel, safe_rows, axis=0).astype(jnp.float32)
    similarity_scores = logit_scale * jnp.sum(query_set.astype(jnp.float32) * target_rows, axis=1)
    factor = jnp.where(owned, positive_weight * (jax.nn.sigmoid(similarity_scores) - 1.0), 0.0)
    query_near = logit_scale * factor[:, None] * target_rows
    panel_near = logit_scale * jax.ops.segment_sum(
        factor[:, None] * query_set.astype(jnp.float32), safe_rows, num_segments=row_total
    )
    return (query_near, panel_near)


def plain_shards(queries, passages, partner, pair_codes, pair_count, positive):
    idx_total = lax.axis_size("idx")
    own_index = lax.axis_index("idx")
    member = lax.axis_index("grp")
    panel_rows = passages.shape[1]
    columns = queries.shape[2]
    pass_total = partner.shape[0]
    logit_scale = columns ** (-0.5)
    inverse = jnp.argsort(partner, axis=1)
    home_queries, home_targets = (
        lax.all_gather(queries, "grp", axis=1, tiled=True),
        lax.all_gather(positive, "grp", axis=1, tiled=True),
    )
    home_set = home_queries[0]
    own_panel = passages[0]
    near_query, near_passage = near_terms(
        home_set, home_targets[0], own_panel, member * panel_rows, logit_scale
    )
    piece_rows = panel_rows // idx_total
    spread = lax.all_to_all(
        own_panel.reshape(idx_total, piece_rows, columns),
        "idx",
        split_axis=0,
        concat_axis=0,
        tiled=True,
    )
    routed = lax.all_to_all(
        jnp.take(spread, partner, axis=0), "idx", split_axis=1, concat_axis=1, tiled=True
    )
    query_acc = near_query
    returned = jnp.zeros((idx_total, piece_rows, columns), jnp.float32)
    for pass_index in range(pass_total):
        query_portion, panel_portion = score_list(
            home_set,
            routed[pass_index].reshape(panel_rows, columns),
            pair_codes[pass_index, own_index, 0],
            pair_count[pass_index, own_index, 0],
            logit_scale,
        )
        query_acc = query_acc + query_portion
        outgoing = panel_portion.astype(jnp.bfloat16).reshape(idx_total, piece_rows, columns)
        arrived = lax.all_to_all(outgoing, "idx", split_axis=0, concat_axis=0, tiled=True)
        returned = returned + jnp.take(arrived, inverse[pass_index], axis=0).astype(jnp.float32)
    far_passage = lax.all_to_all(returned, "idx", split_axis=0, concat_axis=0, tiled=True)
    passage_total = far_passage.reshape(panel_rows, columns) + near_passage
    query_total = lax.psum_scatter(query_acc[None], "grp", scatter_dimension=1, tiled=True)
    return (query_total, passage_total[None])


def dot_nt(a, b):
    return lax.dot_general(a, b, (((1,), (1,)), ((), ())), preferred_element_type=jnp.float32)


def dot_nn(a, b):
    return lax.dot_general(a, b, (((1,), (0,)), ((), ())), preferred_element_type=jnp.float32)


def dot_tn(a, b):
    return lax.dot_general(a, b, (((0,), (0,)), ((), ())), preferred_element_type=jnp.float32)


def fused_kernel(
    n, m, rounds, scale,
    partner_ref, codes_ref, count_ref, q_ref, p_ref, pos_ref,
    qg_ref, pg_ref,
    qall, posall, spread, stage, routed, grads, arrived, fin_out, fin_in,
    part_out, part_in, facc, pacc, wbuf, live,
    spread_send, spread_recv, q_send, q_recv, pos_send, pos_recv,
    route_send, route_recv, back_send, back_recv, fin_send, fin_recv, part_send, part_recv,
):
    me = lax.axis_index("idx")
    mg = lax.axis_index("grp")
    rows, columns = q_ref.shape
    panel_rows = p_ref.shape[0] * p_ref.shape[1]
    slots = codes_ref.shape[2]
    query_blocks, panel_blocks = m * rows // BLK, panel_rows // BLK
    per_rows = rows // BLK

    barrier = pltpu.get_barrier_semaphore()
    for d in range(1, n):
        pl.semaphore_signal(
            barrier, inc=1, device_id={"idx": lax.rem(me + d, n)}, device_id_type=pl.DeviceIdType.MESH
        )
    for d in range(1, m):
        pl.semaphore_signal(
            barrier, inc=1, device_id={"grp": lax.rem(mg + d, m)}, device_id_type=pl.DeviceIdType.MESH
        )
    pl.semaphore_wait(barrier, n + m - 2)

    def idx_copy(src, dst, send, recv, d):
        return pltpu.make_async_remote_copy(
            src_ref=src, dst_ref=dst, send_sem=send, recv_sem=recv,
            device_id={"idx": lax.rem(me + d, n)}, device_id_type=pl.DeviceIdType.MESH,
        )

    def grp_copy(src, dst, send, recv, d):
        return pltpu.make_async_remote_copy(
            src_ref=src, dst_ref=dst, send_sem=send, recv_sem=recv,
            device_id={"grp": lax.rem(mg + d, m)}, device_id_type=pl.DeviceIdType.MESH,
        )

    def spread_copy(d):
        return idx_copy(p_ref.at[lax.rem(me + d, n)], spread.at[me], spread_send.at[d], spread_recv.at[d], d)

    def route_copy(r, d):
        return idx_copy(
            stage.at[r, lax.rem(me + d, n)], routed.at[r, me], route_send.at[r, d], route_recv.at[r, d], d
        )

    def back_copy(r, d):
        return idx_copy(
            grads.at[r, lax.rem(me + d, n)], arrived.at[r, me], back_send.at[r, d], back_recv.at[r, d], d
        )

    def fin_copy(d):
        return idx_copy(fin_out.at[lax.rem(me + d, n)], fin_in.at[me], fin_send.at[d], fin_recv.at[d], d)

    def q_copy(d):
        return grp_copy(q_ref, qall.at[mg], q_send.at[d], q_recv.at[d], d)

    def pos_copy(d):
        return grp_copy(pos_ref, posall.at[mg], pos_send.at[d], pos_recv.at[d], d)

    def part_copy(d):
        return grp_copy(
            part_out.at[lax.rem(mg + d, m)], part_in.at[mg], part_send.at[d], part_recv.at[d], d
        )

    for d in range(1, n):
        spread_copy(d).start()
    for d in range(1, m):
        pos_copy(d).start()
        q_copy(d).start()
    spread[me] = p_ref[me]
    qall[mg] = q_ref[...]
    posall[mg] = pos_ref[...]

    code_at = panel_blocks * lax.broadcasted_iota(jnp.int32, (query_blocks, panel_rows), 0) + (
        lax.broadcasted_iota(jnp.int32, (query_blocks, panel_rows), 1) // BLK
    )
    for r in range(rounds):
        count = count_ref[r, me]
        hit = jnp.zeros((query_blocks, panel_rows), jnp.float32)
        for k in range(slots):
            code = jnp.where(k < count, codes_ref[r, me, k], -1)
            hit = jnp.where(code_at == code, 1.0, hit)
        for block in range(query_blocks):
            live[r, block // per_rows, block % per_rows] = hit[block : block + 1]

    for d in range(1, n):
        spread_copy(d).wait_recv()
    for r in range(rounds):
        for c in range(n):
            stage[r, c] = spread[partner_ref[r, c]]
        for d in range(1, n):
            route_copy(r, d).start()
        routed[r, me] = stage[r, me]

    for d in range(1, m):
        pos_copy(d).wait_recv()
        q_copy(d).wait_recv()

    own = p_ref[...].reshape(panel_rows, columns)
    panel_row = lax.broadcasted_iota(jnp.int32, (panel_rows, rows), 0) + mg * panel_rows
    pg_ref[...] = jnp.zeros(pg_ref.shape, jnp.float32)

    def near_block(h, carry):
        q = qall[h]
        hit = panel_row == posall[h]
        score = scale * jnp.sum(jnp.where(hit, dot_nt(own, q), 0.0), axis=0, keepdims=True)
        coef = positive_weight * (jax.nn.sigmoid(score) - 1.0)
        weight = jnp.where(hit, coef, 0.0)
        high = weight.astype(jnp.bfloat16)
        low = (weight - high.astype(jnp.float32)).astype(jnp.bfloat16)
        pg_ref[...] += dot_nn(high, q) + dot_nn(low, q)
        facc[h] = dot_tn(high, own) + dot_tn(low, own)
        return carry

    lax.fori_loop(0, m, near_block, 0)

    for r in range(rounds):
        for d in range(1, n):
            route_copy(r, d).wait_recv()
        panel = routed[r].reshape(panel_rows, columns)
        pacc[...] = jnp.zeros(pacc.shape, jnp.float32)

        def score_block(h, carry):
            q = qall[h]
            scores = scale * dot_nt(q, panel)
            mask = jnp.concatenate(
                [jnp.broadcast_to(live[r, h, b], (BLK, panel_rows)) for b in range(per_rows)], axis=0
            )
            weight = jnp.where(mask > 0.0, jax.nn.sigmoid(scores), 0.0).astype(jnp.bfloat16)
            wbuf[h] = weight
            pacc[...] += dot_tn(weight, q)
            return carry

        lax.fori_loop(0, m, score_block, 0)
        grads[r] = (scale * pacc[...]).astype(jnp.bfloat16).reshape(grads.shape[1:])
        for d in range(1, n):
            back_copy(r, d).start()
        arrived[r, me] = grads[r, me]

        if r < rounds - 1:
            def query_block(h, carry):
                facc[h] += dot_nn(wbuf[h], panel)
                return carry

            lax.fori_loop(0, m, query_block, 0)
        else:
            def last_block(d, carry):
                h = lax.rem(mg + d, m)
                part_out[h] = (scale * (facc[h] + dot_nn(wbuf[h], panel))).astype(jnp.bfloat16)
                part_copy(d).start()
                return carry

            lax.fori_loop(1, m, last_block, 0)
            qg_ref[...] = scale * (facc[mg] + dot_nn(wbuf[mg], panel))

    for r in range(rounds):
        for d in range(1, n):
            back_copy(r, d).wait_recv()
    for j in range(n):
        total = jnp.zeros(fin_out.shape[1:], jnp.float32)
        for r in range(rounds):
            source = jnp.int32(0)
            for c in range(n):
                source = jnp.where(partner_ref[r, c] == j, c, source)
            total = total + arrived[r, source].astype(jnp.float32)
        fin_out[j] = total.astype(jnp.bfloat16)
    for d in range(1, n):
        fin_copy(d).start()
    fin_in[me] = fin_out[me]

    for d in range(1, m):
        part_copy(d).wait_recv()
        qg_ref[...] += part_in[lax.rem(mg + m - d, m)].astype(jnp.float32)

    for d in range(1, n):
        fin_copy(d).wait_recv()
    pg_ref[...] = scale * pg_ref[...] + fin_in[...].reshape(panel_rows, columns).astype(jnp.float32)

    for d in range(1, n):
        spread_copy(d).wait_send()
        fin_copy(d).wait_send()
        for r in range(rounds):
            route_copy(r, d).wait_send()
            back_copy(r, d).wait_send()
    for d in range(1, m):
        q_copy(d).wait_send()
        pos_copy(d).wait_send()
        part_copy(d).wait_send()


def fused_shards(queries, passages, partner, pair_codes, pair_count, positive):
    n, m = lax.axis_size("idx"), lax.axis_size("grp")
    rounds = partner.shape[0]
    rows, columns = queries.shape[1:]
    panel_rows = passages.shape[1]
    piece = panel_rows // n
    slots = pair_codes.shape[3]
    bf16, f32, dma = jnp.bfloat16, jnp.float32, pltpu.SemaphoreType.DMA
    vmem, smem = pl.BlockSpec(memory_space=pltpu.VMEM), pl.BlockSpec(memory_space=pltpu.SMEM)
    pieces = (n, piece, columns)
    query_grad, passage_grad = pl.pallas_call(
        functools.partial(fused_kernel, n, m, rounds, columns ** (-0.5)),
        out_shape=(
            jax.ShapeDtypeStruct((rows, columns), f32),
            jax.ShapeDtypeStruct((panel_rows, columns), f32),
        ),
        in_specs=[smem] * 3 + [vmem] * 3,
        out_specs=(vmem, vmem),
        scratch_shapes=[
            pltpu.VMEM((m, rows, columns), bf16),
            pltpu.VMEM((m, 1, rows), jnp.int32),
            pltpu.VMEM(pieces, bf16),
            pltpu.VMEM((rounds,) + pieces, bf16),
            pltpu.VMEM((rounds,) + pieces, bf16),
            pltpu.VMEM((rounds,) + pieces, bf16),
            pltpu.VMEM((rounds,) + pieces, bf16),
            pltpu.VMEM(pieces, bf16),
            pltpu.VMEM(pieces, bf16),
            pltpu.VMEM((m, rows, columns), bf16),
            pltpu.VMEM((m, rows, columns), bf16),
            pltpu.VMEM((m, rows, columns), f32),
            pltpu.VMEM((panel_rows, columns), f32),
            pltpu.VMEM((m, rows, panel_rows), bf16),
            pltpu.VMEM((rounds, m, rows // BLK, 1, panel_rows), f32),
            dma((n,)), dma((n,)), dma((m,)), dma((m,)), dma((m,)), dma((m,)),
            dma((rounds, n)), dma((rounds, n)), dma((rounds, n)), dma((rounds, n)),
            dma((n,)), dma((n,)), dma((m,)), dma((m,)),
        ],
        compiler_params=pltpu.CompilerParams(
            collective_id=0, has_side_effects=True, vmem_limit_bytes=40 * 1024 * 1024
        ),
    )(
        partner,
        pair_codes.reshape(rounds, n, slots),
        pair_count.reshape(rounds, n),
        queries[0],
        passages.reshape(pieces),
        positive,
    )
    return (query_grad[None], passage_grad[None])


def shards(queries, passages, partner, pair_codes, pair_count, positive):
    n = lax.axis_size("idx")
    if passages.shape[1] % (16 * n) == 0 and partner.shape[1] == n:
        return fused_shards(queries, passages, partner, pair_codes, pair_count, positive)
    return plain_shards(queries, passages, partner, pair_codes, pair_count, positive)


def solution(mesh):
    in_specs = (
        P("idx", "grp", None),
        P("idx", "grp", None),
        P(),
        P(None, None, "grp", None),
        P(None, None, "grp"),
        P("idx", "grp"),
    )
    out_specs = (P("idx", "grp", None), P("idx", "grp", None))
    return jax.shard_map(shards, mesh=mesh, in_specs=in_specs, out_specs=out_specs, check_vma=False)
```

```python
import functools
import math

import jax
import jax.numpy as jnp
from jax import lax
from jax.experimental import pallas as pl
from jax.experimental.pallas import tpu as pltpu
from jax.sharding import PartitionSpec as P

BLK = 128


positive_weight = 16.0


def score_list(query_set, panel_shard, pair_list, live_count, logit_scale):
    query_tiles = query_set.shape[0] // BLK
    panel_tiles = panel_shard.shape[0] // BLK
    columns = query_set.shape[1]
    slot_total = pair_list.shape[0]
    group_size = math.gcd(48, slot_total)
    query_grid = query_set.reshape(query_tiles, BLK, columns)
    panel_grid = panel_shard.reshape(panel_tiles, BLK, columns)

    def one_group(turn_index, partial_sums):
        query_acc, panel_acc = partial_sums
        first_slot = turn_index * group_size
        live_mask = first_slot + jnp.arange(group_size, dtype=jnp.int32) < live_count
        query_index = pair_list // panel_tiles
        panel_index = pair_list % panel_tiles
        query_block_list = jnp.take(query_grid, query_index, axis=0)
        panel_block_list = jnp.take(panel_grid, panel_index, axis=0)
        similarity_scores = logit_scale * jnp.einsum(
            "wzr,wlr->wzl", query_block_list, panel_block_list, preferred_element_type=jnp.float32
        )
        sample_weights = jnp.where(
            live_mask[:, None, None], jax.nn.sigmoid(similarity_scores), 0.0
        ).astype(jnp.bfloat16)
        query_portion = jnp.einsum(
            "nku,nua->nka", sample_weights, panel_block_list, preferred_element_type=jnp.float32
        )
        panel_portion = jnp.einsum(
            "swc,swj->scj", sample_weights, query_block_list, preferred_element_type=jnp.float32
        )
        query_acc = query_acc + jax.ops.segment_sum(
            query_portion, query_index, num_segments=query_tiles
        )
        panel_acc = panel_acc + jax.ops.segment_sum(
            panel_portion, panel_index, num_segments=panel_tiles
        )
        return (query_acc, panel_acc)

    start_sums = (
        jnp.zeros(query_grid.shape, jnp.float32),
        jnp.zeros(panel_grid.shape, jnp.float32),
    )
    turn_total = slot_total // group_size
    query_acc, panel_acc = lax.fori_loop(0, turn_total, one_group, start_sums)
    return (
        logit_scale * query_acc.reshape(query_set.shape),
        logit_scale * panel_acc.reshape(panel_shard.shape),
    )


def near_terms(query_set, targets, own_panel, row_offset, logit_scale):
    row_total = own_panel.shape[0]
    local_rows = targets - row_offset
    owned = (local_rows >= 0) & (local_rows < row_total)
    safe_rows = jnp.clip(local_rows, 0, row_total - 1)
    target_rows = jnp.take(own_panel, safe_rows, axis=0).astype(jnp.float32)
    similarity_scores = logit_scale * jnp.sum(query_set.astype(jnp.float32) * target_rows, axis=1)
    factor = jnp.where(owned, positive_weight * (jax.nn.sigmoid(similarity_scores) - 1.0), 0.0)
    query_near = logit_scale * factor[:, None] * target_rows
    panel_near = logit_scale * jax.ops.segment_sum(
        factor[:, None] * query_set.astype(jnp.float32), safe_rows, num_segments=row_total
    )
    return (query_near, panel_near)


def plain_shards(queries, passages, partner, pair_codes, pair_count, positive):
    idx_total = lax.axis_size("idx")
    own_index = lax.axis_index("idx")
    member = lax.axis_index("grp")
    panel_rows = passages.shape[1]
    columns = queries.shape[2]
    pass_total = partner.shape[0]
    logit_scale = columns ** (-0.5)
    inverse = jnp.argsort(partner, axis=1)
    home_queries, home_targets = (
        lax.all_gather(queries, "grp", axis=1, tiled=True),
        lax.all_gather(positive, "grp", axis=1, tiled=True),
    )
    home_set = home_queries[0]
    own_panel = passages[0]
    near_query, near_passage = near_terms(
        home_set, home_targets[0], own_panel, member * panel_rows, logit_scale
    )
    piece_rows = panel_rows // idx_total
    spread = lax.all_to_all(
        own_panel.reshape(idx_total, piece_rows, columns),
        "idx",
        split_axis=0,
        concat_axis=0,
        tiled=True,
    )
    routed = lax.all_to_all(
        jnp.take(spread, partner, axis=0), "idx", split_axis=1, concat_axis=1, tiled=True
    )
    query_acc = near_query
    returned = jnp.zeros((idx_total, piece_rows, columns), jnp.float32)
    for pass_index in range(pass_total):
        query_portion, panel_portion = score_list(
            home_set,
            routed[pass_index].reshape(panel_rows, columns),
            pair_codes[pass_index, own_index, 0],
            pair_count[pass_index, own_index, 0],
            logit_scale,
        )
        query_acc = query_acc + query_portion
        outgoing = panel_portion.astype(jnp.bfloat16).reshape(idx_total, piece_rows, columns)
        arrived = lax.all_to_all(outgoing, "idx", split_axis=0, concat_axis=0, tiled=True)
        returned = returned + jnp.take(arrived, inverse[pass_index], axis=0).astype(jnp.float32)
    far_passage = lax.all_to_all(returned, "idx", split_axis=0, concat_axis=0, tiled=True)
    passage_total = far_passage.reshape(panel_rows, columns) + near_passage
    query_total = lax.psum_scatter(query_acc[None], "grp", scatter_dimension=1, tiled=True)
    return (query_total, passage_total[None])


def dot_nt(a, b):
    return lax.dot_general(a, b, (((1,), (1,)), ((), ())), preferred_element_type=jnp.float32)


def dot_nn(a, b):
    return lax.dot_general(a, b, (((1,), (0,)), ((), ())), preferred_element_type=jnp.float32)


def dot_tn(a, b):
    return lax.dot_general(a, b, (((0,), (0,)), ((), ())), preferred_element_type=jnp.float32)


def fused_kernel(
    n, m, rounds, scale,
    partner_ref, codes_ref, count_ref, q_ref, p_ref, pos_ref,
    qg_ref, pg_ref,
    qall, posall, spread, stage, routed, grads, arrived, fin_out, fin_in,
    part_out, part_in, facc, pacc, wbuf, live, own_panel, local_sem,
    spread_send, spread_recv, q_send, q_recv, pos_send, pos_recv,
    route_send, route_recv, back_send, back_recv, fin_send, fin_recv, part_send, part_recv,
):
    me = lax.axis_index("idx")
    mg = lax.axis_index("grp")
    rows, columns = q_ref.shape
    panel_rows = p_ref.shape[0] * p_ref.shape[1]
    slots = codes_ref.shape[2]
    query_blocks, panel_blocks = m * rows // BLK, panel_rows // BLK
    per_rows = rows // BLK

    local = [
        pltpu.make_async_copy(p_ref.at[me], spread.at[me], local_sem.at[0]),
        pltpu.make_async_copy(q_ref, qall.at[mg], local_sem.at[1]),
        pltpu.make_async_copy(p_ref, own_panel, local_sem.at[2]),
    ]
    for copy in local:
        copy.start()

    barrier = pltpu.get_barrier_semaphore()
    for d in range(1, n):
        pl.semaphore_signal(
            barrier, inc=1, device_id={"idx": lax.rem(me + d, n)}, device_id_type=pl.DeviceIdType.MESH
        )
    for d in range(1, m):
        pl.semaphore_signal(
            barrier, inc=1, device_id={"grp": lax.rem(mg + d, m)}, device_id_type=pl.DeviceIdType.MESH
        )
    pl.semaphore_wait(barrier, n + m - 2)

    def idx_copy(src, dst, send, recv, d):
        return pltpu.make_async_remote_copy(
            src_ref=src, dst_ref=dst, send_sem=send, recv_sem=recv,
            device_id={"idx": lax.rem(me + d, n)}, device_id_type=pl.DeviceIdType.MESH,
        )

    def grp_copy(src, dst, send, recv, d):
        return pltpu.make_async_remote_copy(
            src_ref=src, dst_ref=dst, send_sem=send, recv_sem=recv,
            device_id={"grp": lax.rem(mg + d, m)}, device_id_type=pl.DeviceIdType.MESH,
        )

    def spread_copy(d):
        return idx_copy(p_ref.at[lax.rem(me + d, n)], spread.at[me], spread_send.at[d], spread_recv.at[d], d)

    def route_copy(r, d):
        return idx_copy(
            stage.at[r, lax.rem(me + d, n)], routed.at[r, me], route_send.at[r, d], route_recv.at[r, d], d
        )

    def back_copy(r, d):
        return idx_copy(
            grads.at[r, lax.rem(me + d, n)], arrived.at[r, me], back_send.at[r, d], back_recv.at[r, d], d
        )

    def fin_copy(d):
        return idx_copy(fin_out.at[lax.rem(me + d, n)], fin_in.at[me], fin_send.at[d], fin_recv.at[d], d)

    def q_copy(d):
        return grp_copy(q_ref, qall.at[mg], q_send.at[d], q_recv.at[d], d)

    def pos_copy(d):
        return grp_copy(pos_ref, posall.at[mg], pos_send.at[d], pos_recv.at[d], d)

    def part_copy(d):
        return grp_copy(
            part_out.at[lax.rem(mg + d, m)], part_in.at[mg], part_send.at[d], part_recv.at[d], d
        )

    for d in range(1, n):
        spread_copy(d).start()
    for d in range(1, m):
        pos_copy(d).start()
        q_copy(d).start()
    posall[mg] = pos_ref[...]

    code_at = panel_blocks * lax.broadcasted_iota(jnp.int32, (query_blocks, panel_rows), 0) + (
        lax.broadcasted_iota(jnp.int32, (query_blocks, panel_rows), 1) // BLK
    )
    for r in range(rounds):
        count = count_ref[r, me]
        hit = jnp.zeros((query_blocks, panel_rows), jnp.float32)
        for k in range(slots):
            code = jnp.where(k < count, codes_ref[r, me, k], -1)
            hit = jnp.where(code_at == code, 1.0, hit)
        for block in range(query_blocks):
            live[r, block // per_rows, block % per_rows] = hit[block : block + 1]

    for copy in local:
        copy.wait()
    for d in range(1, n):
        spread_copy(d).wait_recv()
    for r in range(rounds):
        for c in range(n):
            stage[r, c] = spread[partner_ref[r, c]]
        for d in range(1, n):
            if r > 0:
                route_copy(r - 1, d).wait_send()
            route_copy(r, d).start()
        routed[r, me] = stage[r, me]

    for d in range(1, m):
        pos_copy(d).wait_recv()
        q_copy(d).wait_recv()

    own = own_panel[...].reshape(panel_rows, columns)
    panel_row = lax.broadcasted_iota(jnp.int32, (panel_rows, rows), 0) + mg * panel_rows
    pg_ref[...] = jnp.zeros(pg_ref.shape, jnp.float32)

    def near_block(h, carry):
        q = qall[h]
        hit = panel_row == posall[h]
        score = scale * jnp.sum(jnp.where(hit, dot_nt(own, q), 0.0), axis=0, keepdims=True)
        coef = positive_weight * (jax.nn.sigmoid(score) - 1.0)
        weight = jnp.where(hit, coef, 0.0)
        high = weight.astype(jnp.bfloat16)
        low = (weight - high.astype(jnp.float32)).astype(jnp.bfloat16)
        pg_ref[...] += dot_nn(high, q) + dot_nn(low, q)
        facc[h] = dot_tn(high, own) + dot_tn(low, own)
        return carry

    for r in range(rounds):
        for d in range(1, n):
            route_copy(r, d).wait_recv()
        panel = routed[r].reshape(panel_rows, columns)
        pacc[...] = jnp.zeros(pacc.shape, jnp.float32)

        def score_block(h, carry):
            q = qall[h]
            scores = scale * dot_nt(q, panel)
            mask = jnp.concatenate(
                [jnp.broadcast_to(live[r, h, b], (BLK, panel_rows)) for b in range(per_rows)], axis=0
            )
            weight = jnp.where(mask > 0.0, jax.nn.sigmoid(scores), 0.0).astype(jnp.bfloat16)
            wbuf[h] = weight
            pacc[...] += dot_tn(weight, q)
            return carry

        lax.fori_loop(0, m, score_block, 0)
        grads[r] = (scale * pacc[...]).astype(jnp.bfloat16).reshape(grads.shape[1:])
        for d in range(1, n):
            back_copy(r, d).start()
        arrived[r, me] = grads[r, me]

        if r == 0:
            lax.fori_loop(0, m, near_block, 0)

        if r < rounds - 1:
            def query_block(h, carry):
                facc[h] += dot_nn(wbuf[h], panel)
                return carry

            lax.fori_loop(0, m, query_block, 0)
        else:
            def last_block(d, carry):
                h = lax.rem(mg + d, m)
                part_out[h] = (scale * (facc[h] + dot_nn(wbuf[h], panel))).astype(jnp.bfloat16)
                part_copy(d).start()
                return carry

            lax.fori_loop(1, m, last_block, 0)
            qg_ref[...] = scale * (facc[mg] + dot_nn(wbuf[mg], panel))

    for r in range(rounds):
        for d in range(1, n):
            back_copy(r, d).wait_recv()
    for j in range(n):
        total = jnp.zeros(fin_out.shape[1:], jnp.float32)
        for r in range(rounds):
            source = jnp.int32(0)
            for c in range(n):
                source = jnp.where(partner_ref[r, c] == j, c, source)
            total = total + arrived[r, source].astype(jnp.float32)
        fin_out[j] = total.astype(jnp.bfloat16)
    for d in range(1, n):
        fin_copy(d).start()
    fin_in[me] = fin_out[me]

    for d in range(1, m):
        part_copy(d).wait_recv()
        qg_ref[...] += part_in[lax.rem(mg + m - d, m)].astype(jnp.float32)

    for d in range(1, n):
        fin_copy(d).wait_recv()
    pg_ref[...] = scale * pg_ref[...] + fin_in[...].reshape(panel_rows, columns).astype(jnp.float32)

    for d in range(1, n):
        spread_copy(d).wait_send()
        route_copy(rounds - 1, d).wait_send()
        fin_copy(d).wait_send()
        for r in range(rounds):
            back_copy(r, d).wait_send()
    for d in range(1, m):
        q_copy(d).wait_send()
        pos_copy(d).wait_send()
        part_copy(d).wait_send()


def fused_shards(queries, passages, partner, pair_codes, pair_count, positive):
    n, m = lax.axis_size("idx"), lax.axis_size("grp")
    rounds = partner.shape[0]
    rows, columns = queries.shape[1:]
    panel_rows = passages.shape[1]
    piece = panel_rows // n
    slots = pair_codes.shape[3]
    bf16, f32, dma = jnp.bfloat16, jnp.float32, pltpu.SemaphoreType.DMA
    vmem, smem = pl.BlockSpec(memory_space=pltpu.VMEM), pl.BlockSpec(memory_space=pltpu.SMEM)
    hbm = pl.BlockSpec(memory_space=pl.ANY)
    pieces = (n, piece, columns)
    query_grad, passage_grad = pl.pallas_call(
        functools.partial(fused_kernel, n, m, rounds, columns ** (-0.5)),
        out_shape=(
            jax.ShapeDtypeStruct((rows, columns), f32),
            jax.ShapeDtypeStruct((panel_rows, columns), f32),
        ),
        in_specs=[smem] * 3 + [hbm] * 2 + [vmem],
        out_specs=(vmem, vmem),
        scratch_shapes=[
            pltpu.VMEM((m, rows, columns), bf16),
            pltpu.VMEM((m, 1, rows), jnp.int32),
            pltpu.VMEM(pieces, bf16),
            pltpu.VMEM((rounds,) + pieces, bf16),
            pltpu.VMEM((rounds,) + pieces, bf16),
            pltpu.VMEM((rounds,) + pieces, bf16),
            pltpu.VMEM((rounds,) + pieces, bf16),
            pltpu.VMEM(pieces, bf16),
            pltpu.VMEM(pieces, bf16),
            pltpu.VMEM((m, rows, columns), bf16),
            pltpu.VMEM((m, rows, columns), bf16),
            pltpu.VMEM((m, rows, columns), f32),
            pltpu.VMEM((panel_rows, columns), f32),
            pltpu.VMEM((m, rows, panel_rows), bf16),
            pltpu.VMEM((rounds, m, rows // BLK, 1, panel_rows), f32),
            pltpu.VMEM(pieces, bf16),
            dma((3,)),
            dma((n,)), dma((n,)), dma((m,)), dma((m,)), dma((m,)), dma((m,)),
            dma((rounds, n)), dma((rounds, n)), dma((rounds, n)), dma((rounds, n)),
            dma((n,)), dma((n,)), dma((m,)), dma((m,)),
        ],
        compiler_params=pltpu.CompilerParams(
            collective_id=0, has_side_effects=True, vmem_limit_bytes=56 * 1024 * 1024
        ),
    )(
        partner,
        pair_codes.reshape(rounds, n, slots),
        pair_count.reshape(rounds, n),
        queries[0],
        passages.reshape(pieces),
        positive,
    )
    return (query_grad[None], passage_grad[None])


def shards(queries, passages, partner, pair_codes, pair_count, positive):
    n = lax.axis_size("idx")
    if passages.shape[1] % (16 * n) == 0 and partner.shape[1] == n:
        return fused_shards(queries, passages, partner, pair_codes, pair_count, positive)
    return plain_shards(queries, passages, partner, pair_codes, pair_count, positive)


def solution(mesh):
    in_specs = (
        P("idx", "grp", None),
        P("idx", "grp", None),
        P(),
        P(None, None, "grp", None),
        P(None, None, "grp"),
        P("idx", "grp"),
    )
    out_specs = (P("idx", "grp", None), P("idx", "grp", None))
    return jax.shard_map(shards, mesh=mesh, in_specs=in_specs, out_specs=out_specs, check_vma=False)
```

```python
import functools
import math

import jax
import jax.numpy as jnp
from jax import lax
from jax.experimental import pallas as pl
from jax.experimental.pallas import tpu as pltpu
from jax.sharding import PartitionSpec as P

BLK = 128


positive_weight = 16.0


def score_list(query_set, panel_shard, pair_list, live_count, logit_scale):
    query_tiles = query_set.shape[0] // BLK
    panel_tiles = panel_shard.shape[0] // BLK
    columns = query_set.shape[1]
    slot_total = pair_list.shape[0]
    group_size = math.gcd(48, slot_total)
    query_grid = query_set.reshape(query_tiles, BLK, columns)
    panel_grid = panel_shard.reshape(panel_tiles, BLK, columns)

    def one_group(turn_index, partial_sums):
        query_acc, panel_acc = partial_sums
        first_slot = turn_index * group_size
        live_mask = first_slot + jnp.arange(group_size, dtype=jnp.int32) < live_count
        query_index = pair_list // panel_tiles
        panel_index = pair_list % panel_tiles
        query_block_list = jnp.take(query_grid, query_index, axis=0)
        panel_block_list = jnp.take(panel_grid, panel_index, axis=0)
        similarity_scores = logit_scale * jnp.einsum(
            "wzr,wlr->wzl", query_block_list, panel_block_list, preferred_element_type=jnp.float32
        )
        sample_weights = jnp.where(
            live_mask[:, None, None], jax.nn.sigmoid(similarity_scores), 0.0
        ).astype(jnp.bfloat16)
        query_portion = jnp.einsum(
            "nku,nua->nka", sample_weights, panel_block_list, preferred_element_type=jnp.float32
        )
        panel_portion = jnp.einsum(
            "swc,swj->scj", sample_weights, query_block_list, preferred_element_type=jnp.float32
        )
        query_acc = query_acc + jax.ops.segment_sum(
            query_portion, query_index, num_segments=query_tiles
        )
        panel_acc = panel_acc + jax.ops.segment_sum(
            panel_portion, panel_index, num_segments=panel_tiles
        )
        return (query_acc, panel_acc)

    start_sums = (
        jnp.zeros(query_grid.shape, jnp.float32),
        jnp.zeros(panel_grid.shape, jnp.float32),
    )
    turn_total = slot_total // group_size
    query_acc, panel_acc = lax.fori_loop(0, turn_total, one_group, start_sums)
    return (
        logit_scale * query_acc.reshape(query_set.shape),
        logit_scale * panel_acc.reshape(panel_shard.shape),
    )


def near_terms(query_set, targets, own_panel, row_offset, logit_scale):
    row_total = own_panel.shape[0]
    local_rows = targets - row_offset
    owned = (local_rows >= 0) & (local_rows < row_total)
    safe_rows = jnp.clip(local_rows, 0, row_total - 1)
    target_rows = jnp.take(own_panel, safe_rows, axis=0).astype(jnp.float32)
    similarity_scores = logit_scale * jnp.sum(query_set.astype(jnp.float32) * target_rows, axis=1)
    factor = jnp.where(owned, positive_weight * (jax.nn.sigmoid(similarity_scores) - 1.0), 0.0)
    query_near = logit_scale * factor[:, None] * target_rows
    panel_near = logit_scale * jax.ops.segment_sum(
        factor[:, None] * query_set.astype(jnp.float32), safe_rows, num_segments=row_total
    )
    return (query_near, panel_near)


def plain_shards(queries, passages, partner, pair_codes, pair_count, positive):
    idx_total = lax.axis_size("idx")
    own_index = lax.axis_index("idx")
    member = lax.axis_index("grp")
    panel_rows = passages.shape[1]
    columns = queries.shape[2]
    pass_total = partner.shape[0]
    logit_scale = columns ** (-0.5)
    inverse = jnp.argsort(partner, axis=1)
    home_queries, home_targets = (
        lax.all_gather(queries, "grp", axis=1, tiled=True),
        lax.all_gather(positive, "grp", axis=1, tiled=True),
    )
    home_set = home_queries[0]
    own_panel = passages[0]
    near_query, near_passage = near_terms(
        home_set, home_targets[0], own_panel, member * panel_rows, logit_scale
    )
    piece_rows = panel_rows // idx_total
    spread = lax.all_to_all(
        own_panel.reshape(idx_total, piece_rows, columns),
        "idx",
        split_axis=0,
        concat_axis=0,
        tiled=True,
    )
    routed = lax.all_to_all(
        jnp.take(spread, partner, axis=0), "idx", split_axis=1, concat_axis=1, tiled=True
    )
    query_acc = near_query
    returned = jnp.zeros((idx_total, piece_rows, columns), jnp.float32)
    for pass_index in range(pass_total):
        query_portion, panel_portion = score_list(
            home_set,
            routed[pass_index].reshape(panel_rows, columns),
            pair_codes[pass_index, own_index, 0],
            pair_count[pass_index, own_index, 0],
            logit_scale,
        )
        query_acc = query_acc + query_portion
        outgoing = panel_portion.astype(jnp.bfloat16).reshape(idx_total, piece_rows, columns)
        arrived = lax.all_to_all(outgoing, "idx", split_axis=0, concat_axis=0, tiled=True)
        returned = returned + jnp.take(arrived, inverse[pass_index], axis=0).astype(jnp.float32)
    far_passage = lax.all_to_all(returned, "idx", split_axis=0, concat_axis=0, tiled=True)
    passage_total = far_passage.reshape(panel_rows, columns) + near_passage
    query_total = lax.psum_scatter(query_acc[None], "grp", scatter_dimension=1, tiled=True)
    return (query_total, passage_total[None])


def dot_nt(a, b):
    return lax.dot_general(a, b, (((1,), (1,)), ((), ())), preferred_element_type=jnp.float32)


def dot_nn(a, b):
    return lax.dot_general(a, b, (((1,), (0,)), ((), ())), preferred_element_type=jnp.float32)


def dot_tn(a, b):
    return lax.dot_general(a, b, (((0,), (0,)), ((), ())), preferred_element_type=jnp.float32)


def fused_kernel(
    n, m, rounds, scale,
    partner_ref, codes_ref, count_ref, q_ref, p_ref, pos_ref,
    qg_ref, pg_ref,
    qall, posall, spread_a, spread_b, stage, routed, grads, arrived, last_a, last_b, fin_out, fin_in,
    part_out, part_in, facc, pacc, wbuf, live, own_panel, local_sem,
    spread_send, spread_recv, q_send, q_recv, pos_send, pos_recv,
    route_send, route_recv, back_send, back_recv, fin_send, fin_recv, part_send, part_recv,
):
    me = lax.axis_index("idx")
    mg = lax.axis_index("grp")
    rows, columns = q_ref.shape
    panel_rows = p_ref.shape[0] * p_ref.shape[1]
    slots = codes_ref.shape[2]
    query_blocks, panel_blocks = m * rows // BLK, panel_rows // BLK
    per_rows = rows // BLK
    piece = p_ref.shape[1]
    spread, last = (spread_a, spread_b), (last_a, last_b)
    chunks = len(spread)
    steps = sorted(range(1, n), key=lambda d: -min(d, n - d))

    def route_parts(r):
        return chunks if r == 0 else 1

    def back_parts(r):
        return chunks if r == rounds - 1 else 1

    def part_rows(h, parts):
        return pl.ds(h * (piece // parts), piece // parts)

    local = [
        pltpu.make_async_copy(q_ref, qall.at[mg], local_sem.at[0]),
        pltpu.make_async_copy(p_ref, own_panel, local_sem.at[1]),
    ] + [
        pltpu.make_async_copy(
            p_ref.at[me, part_rows(h, chunks)], spread[h].at[me], local_sem.at[2 + h]
        )
        for h in range(chunks)
    ]
    for copy in local:
        copy.start()

    barrier = pltpu.get_barrier_semaphore()
    for d in range(1, n):
        pl.semaphore_signal(
            barrier, inc=1, device_id={"idx": lax.rem(me + d, n)}, device_id_type=pl.DeviceIdType.MESH
        )
    for d in range(1, m):
        pl.semaphore_signal(
            barrier, inc=1, device_id={"grp": lax.rem(mg + d, m)}, device_id_type=pl.DeviceIdType.MESH
        )
    pl.semaphore_wait(barrier, n + m - 2)

    def idx_copy(src, dst, send, recv, d):
        return pltpu.make_async_remote_copy(
            src_ref=src, dst_ref=dst, send_sem=send, recv_sem=recv,
            device_id={"idx": lax.rem(me + d, n)}, device_id_type=pl.DeviceIdType.MESH,
        )

    def grp_copy(src, dst, send, recv, d):
        return pltpu.make_async_remote_copy(
            src_ref=src, dst_ref=dst, send_sem=send, recv_sem=recv,
            device_id={"grp": lax.rem(mg + d, m)}, device_id_type=pl.DeviceIdType.MESH,
        )

    def spread_copy(h, d):
        span = part_rows(h, chunks)
        return idx_copy(
            p_ref.at[lax.rem(me + d, n), span], spread[h].at[me],
            spread_send.at[h, d], spread_recv.at[h, d], d,
        )

    def route_copy(r, h, d):
        span = part_rows(h, route_parts(r))
        return idx_copy(
            stage.at[r, lax.rem(me + d, n), span], routed.at[r, me, span],
            route_send.at[r, h, d], route_recv.at[r, h, d], d,
        )

    def back_copy(r, h, d):
        span = part_rows(h, back_parts(r))
        return idx_copy(
            grads.at[r, lax.rem(me + d, n), span],
            last[h].at[me] if r == rounds - 1 else arrived.at[r, me],
            back_send.at[r, h, d], back_recv.at[r, h, d], d,
        )

    def fin_copy(h, d):
        span = part_rows(h, chunks)
        return idx_copy(
            fin_out.at[lax.rem(me + d, n), span], fin_in.at[me, span],
            fin_send.at[h, d], fin_recv.at[h, d], d,
        )

    def q_copy(d):
        return grp_copy(q_ref, qall.at[mg], q_send.at[d], q_recv.at[d], d)

    def pos_copy(d):
        return grp_copy(pos_ref, posall.at[mg], pos_send.at[d], pos_recv.at[d], d)

    def part_copy(d):
        return grp_copy(
            part_out.at[lax.rem(mg + d, m)], part_in.at[mg], part_send.at[d], part_recv.at[d], d
        )

    for h in range(chunks):
        for d in steps:
            spread_copy(h, d).start()
    for d in range(1, m):
        pos_copy(d).start()
        q_copy(d).start()
    posall[mg] = pos_ref[...]

    code_at = panel_blocks * lax.broadcasted_iota(jnp.int32, (query_blocks, panel_rows), 0) + (
        lax.broadcasted_iota(jnp.int32, (query_blocks, panel_rows), 1) // BLK
    )
    for r in range(rounds):
        count = count_ref[r, me]
        hit = jnp.zeros((query_blocks, panel_rows), jnp.float32)
        for k in range(slots):
            code = jnp.where(k < count, codes_ref[r, me, k], -1)
            hit = jnp.where(code_at == code, 1.0, hit)
        for block in range(query_blocks):
            live[r, block // per_rows, block % per_rows] = hit[block : block + 1]

    for copy in local:
        copy.wait()
    for h in range(chunks):
        span = part_rows(h, chunks)
        for d in steps:
            spread_copy(h, d).wait_recv()
        for c in range(n):
            stage[0, c, span] = spread[h][partner_ref[0, c]]
        for d in steps:
            route_copy(0, h, d).start()
    routed[0, me] = stage[0, me]
    for r in range(1, rounds):
        for c in range(n):
            for h in range(chunks):
                stage[r, c, part_rows(h, chunks)] = spread[h][partner_ref[r, c]]
        for d in steps:
            for h in range(route_parts(r - 1)):
                route_copy(r - 1, h, d).wait_send()
            route_copy(r, 0, d).start()
        routed[r, me] = stage[r, me]

    for d in range(1, m):
        pos_copy(d).wait_recv()
        q_copy(d).wait_recv()

    own = own_panel[...].reshape(panel_rows, columns)
    panel_row = lax.broadcasted_iota(jnp.int32, (panel_rows, rows), 0) + mg * panel_rows
    pg_ref[...] = jnp.zeros(pg_ref.shape, jnp.float32)

    def near_block(h, carry):
        q = qall[h]
        hit = panel_row == posall[h]
        score = scale * jnp.sum(jnp.where(hit, dot_nt(own, q), 0.0), axis=0, keepdims=True)
        coef = positive_weight * (jax.nn.sigmoid(score) - 1.0)
        weight = jnp.where(hit, coef, 0.0)
        high = weight.astype(jnp.bfloat16)
        low = (weight - high.astype(jnp.float32)).astype(jnp.bfloat16)
        pg_ref[...] += dot_nn(high, q) + dot_nn(low, q)
        facc[h] = dot_tn(high, own) + dot_tn(low, own)
        return carry

    for r in range(rounds):
        for h in range(route_parts(r)):
            for d in steps:
                route_copy(r, h, d).wait_recv()
        panel = routed[r].reshape(panel_rows, columns)
        pacc[...] = jnp.zeros(pacc.shape, jnp.float32)

        def score_block(h, carry):
            q = qall[h]
            scores = scale * dot_nt(q, panel)
            mask = jnp.concatenate(
                [jnp.broadcast_to(live[r, h, b], (BLK, panel_rows)) for b in range(per_rows)], axis=0
            )
            weight = jnp.where(mask > 0.0, jax.nn.sigmoid(scores), 0.0).astype(jnp.bfloat16)
            wbuf[h] = weight
            pacc[...] += dot_tn(weight, q)
            return carry

        lax.fori_loop(0, m, score_block, 0)
        grads[r] = (scale * pacc[...]).astype(jnp.bfloat16).reshape(grads.shape[1:])
        for h in range(back_parts(r)):
            for d in steps:
                back_copy(r, h, d).start()
        if r < rounds - 1:
            arrived[r, me] = grads[r, me]
        else:
            for h in range(chunks):
                last[h][me] = grads[r, me, part_rows(h, chunks)]

        if r == 0:
            lax.fori_loop(0, m, near_block, 0)

        if r < rounds - 1:
            def query_block(h, carry):
                facc[h] += dot_nn(wbuf[h], panel)
                return carry

            lax.fori_loop(0, m, query_block, 0)
        else:
            def last_block(d, carry):
                h = lax.rem(mg + d, m)
                part_out[h] = (scale * (facc[h] + dot_nn(wbuf[h], panel))).astype(jnp.bfloat16)
                part_copy(d).start()
                return carry

            lax.fori_loop(1, m, last_block, 0)
            qg_ref[...] = scale * (facc[mg] + dot_nn(wbuf[mg], panel))

    for r in range(rounds - 1):
        for d in steps:
            back_copy(r, 0, d).wait_recv()
    sources = []
    for r in range(rounds):
        for j in range(n):
            source = jnp.int32(0)
            for c in range(n):
                source = jnp.where(partner_ref[r, c] == j, c, source)
            sources.append(source)
    for h in range(chunks):
        span = part_rows(h, chunks)
        for d in steps:
            back_copy(rounds - 1, h, d).wait_recv()
        for j in range(n):
            total = last[h][sources[(rounds - 1) * n + j]].astype(jnp.float32)
            for r in range(rounds - 1):
                total = total + arrived[r, sources[r * n + j], span].astype(jnp.float32)
            fin_out[j, span] = total.astype(jnp.bfloat16)
        for d in steps:
            fin_copy(h, d).start()
    fin_in[me] = fin_out[me]

    for d in range(1, m):
        part_copy(d).wait_recv()
        qg_ref[...] += part_in[lax.rem(mg + m - d, m)].astype(jnp.float32)

    for h in range(chunks):
        for d in steps:
            fin_copy(h, d).wait_recv()
    pg_ref[...] = scale * pg_ref[...] + fin_in[...].reshape(panel_rows, columns).astype(jnp.float32)

    for d in steps:
        for h in range(chunks):
            spread_copy(h, d).wait_send()
            fin_copy(h, d).wait_send()
        for h in range(route_parts(rounds - 1)):
            route_copy(rounds - 1, h, d).wait_send()
        for r in range(rounds):
            for h in range(back_parts(r)):
                back_copy(r, h, d).wait_send()
    for d in range(1, m):
        q_copy(d).wait_send()
        pos_copy(d).wait_send()
        part_copy(d).wait_send()


def fused_shards(queries, passages, partner, pair_codes, pair_count, positive):
    n, m = lax.axis_size("idx"), lax.axis_size("grp")
    rounds = partner.shape[0]
    rows, columns = queries.shape[1:]
    panel_rows = passages.shape[1]
    piece = panel_rows // n
    slots = pair_codes.shape[3]
    bf16, f32, dma = jnp.bfloat16, jnp.float32, pltpu.SemaphoreType.DMA
    vmem, smem = pl.BlockSpec(memory_space=pltpu.VMEM), pl.BlockSpec(memory_space=pltpu.SMEM)
    hbm = pl.BlockSpec(memory_space=pl.ANY)
    pieces, halves = (n, piece, columns), (n, piece // 2, columns)
    query_grad, passage_grad = pl.pallas_call(
        functools.partial(fused_kernel, n, m, rounds, columns ** (-0.5)),
        out_shape=(
            jax.ShapeDtypeStruct((rows, columns), f32),
            jax.ShapeDtypeStruct((panel_rows, columns), f32),
        ),
        in_specs=[smem] * 3 + [hbm] * 2 + [vmem],
        out_specs=(vmem, vmem),
        scratch_shapes=[
            pltpu.VMEM((m, rows, columns), bf16),
            pltpu.VMEM((m, 1, rows), jnp.int32),
            pltpu.VMEM(halves, bf16),
            pltpu.VMEM(halves, bf16),
            pltpu.VMEM((rounds,) + pieces, bf16),
            pltpu.VMEM((rounds,) + pieces, bf16),
            pltpu.VMEM((rounds,) + pieces, bf16),
            pltpu.VMEM((max(rounds - 1, 1),) + pieces, bf16),
            pltpu.VMEM(halves, bf16),
            pltpu.VMEM(halves, bf16),
            pltpu.VMEM(pieces, bf16),
            pltpu.VMEM(pieces, bf16),
            pltpu.VMEM((m, rows, columns), bf16),
            pltpu.VMEM((m, rows, columns), bf16),
            pltpu.VMEM((m, rows, columns), f32),
            pltpu.VMEM((panel_rows, columns), f32),
            pltpu.VMEM((m, rows, panel_rows), bf16),
            pltpu.VMEM((rounds, m, rows // BLK, 1, panel_rows), f32),
            pltpu.VMEM(pieces, bf16),
            dma((4,)),
            dma((2, n)), dma((2, n)), dma((m,)), dma((m,)), dma((m,)), dma((m,)),
            dma((rounds, 2, n)), dma((rounds, 2, n)), dma((rounds, 2, n)), dma((rounds, 2, n)),
            dma((2, n)), dma((2, n)), dma((m,)), dma((m,)),
        ],
        compiler_params=pltpu.CompilerParams(
            collective_id=0, has_side_effects=True, vmem_limit_bytes=56 * 1024 * 1024
        ),
    )(
        partner,
        pair_codes.reshape(rounds, n, slots),
        pair_count.reshape(rounds, n),
        queries[0],
        passages.reshape(pieces),
        positive,
    )
    return (query_grad[None], passage_grad[None])


def shards(queries, passages, partner, pair_codes, pair_count, positive):
    n = lax.axis_size("idx")
    if passages.shape[1] % (32 * n) == 0 and partner.shape[1] == n:
        return fused_shards(queries, passages, partner, pair_codes, pair_count, positive)
    return plain_shards(queries, passages, partner, pair_codes, pair_count, positive)


def solution(mesh):
    in_specs = (
        P("idx", "grp", None),
        P("idx", "grp", None),
        P(),
        P(None, None, "grp", None),
        P(None, None, "grp"),
        P("idx", "grp"),
    )
    out_specs = (P("idx", "grp", None), P("idx", "grp", None))
    return jax.shard_map(shards, mesh=mesh, in_specs=in_specs, out_specs=out_specs, check_vma=False)
```

```python
import functools
import math

import jax
import jax.numpy as jnp
from jax import lax
from jax.experimental import pallas as pl
from jax.experimental.pallas import tpu as pltpu
from jax.sharding import PartitionSpec as P

BLK = 128


positive_weight = 16.0


def score_list(query_set, panel_shard, pair_list, live_count, logit_scale):
    query_tiles = query_set.shape[0] // BLK
    panel_tiles = panel_shard.shape[0] // BLK
    columns = query_set.shape[1]
    slot_total = pair_list.shape[0]
    group_size = math.gcd(48, slot_total)
    query_grid = query_set.reshape(query_tiles, BLK, columns)
    panel_grid = panel_shard.reshape(panel_tiles, BLK, columns)

    def one_group(turn_index, partial_sums):
        query_acc, panel_acc = partial_sums
        first_slot = turn_index * group_size
        live_mask = first_slot + jnp.arange(group_size, dtype=jnp.int32) < live_count
        query_index = pair_list // panel_tiles
        panel_index = pair_list % panel_tiles
        query_block_list = jnp.take(query_grid, query_index, axis=0)
        panel_block_list = jnp.take(panel_grid, panel_index, axis=0)
        similarity_scores = logit_scale * jnp.einsum(
            "wzr,wlr->wzl", query_block_list, panel_block_list, preferred_element_type=jnp.float32
        )
        sample_weights = jnp.where(
            live_mask[:, None, None], jax.nn.sigmoid(similarity_scores), 0.0
        ).astype(jnp.bfloat16)
        query_portion = jnp.einsum(
            "nku,nua->nka", sample_weights, panel_block_list, preferred_element_type=jnp.float32
        )
        panel_portion = jnp.einsum(
            "swc,swj->scj", sample_weights, query_block_list, preferred_element_type=jnp.float32
        )
        query_acc = query_acc + jax.ops.segment_sum(
            query_portion, query_index, num_segments=query_tiles
        )
        panel_acc = panel_acc + jax.ops.segment_sum(
            panel_portion, panel_index, num_segments=panel_tiles
        )
        return (query_acc, panel_acc)

    start_sums = (
        jnp.zeros(query_grid.shape, jnp.float32),
        jnp.zeros(panel_grid.shape, jnp.float32),
    )
    turn_total = slot_total // group_size
    query_acc, panel_acc = lax.fori_loop(0, turn_total, one_group, start_sums)
    return (
        logit_scale * query_acc.reshape(query_set.shape),
        logit_scale * panel_acc.reshape(panel_shard.shape),
    )


def near_terms(query_set, targets, own_panel, row_offset, logit_scale):
    row_total = own_panel.shape[0]
    local_rows = targets - row_offset
    owned = (local_rows >= 0) & (local_rows < row_total)
    safe_rows = jnp.clip(local_rows, 0, row_total - 1)
    target_rows = jnp.take(own_panel, safe_rows, axis=0).astype(jnp.float32)
    similarity_scores = logit_scale * jnp.sum(query_set.astype(jnp.float32) * target_rows, axis=1)
    factor = jnp.where(owned, positive_weight * (jax.nn.sigmoid(similarity_scores) - 1.0), 0.0)
    query_near = logit_scale * factor[:, None] * target_rows
    panel_near = logit_scale * jax.ops.segment_sum(
        factor[:, None] * query_set.astype(jnp.float32), safe_rows, num_segments=row_total
    )
    return (query_near, panel_near)


def plain_shards(queries, passages, partner, pair_codes, pair_count, positive):
    idx_total = lax.axis_size("idx")
    own_index = lax.axis_index("idx")
    member = lax.axis_index("grp")
    panel_rows = passages.shape[1]
    columns = queries.shape[2]
    pass_total = partner.shape[0]
    logit_scale = columns ** (-0.5)
    inverse = jnp.argsort(partner, axis=1)
    home_queries, home_targets = (
        lax.all_gather(queries, "grp", axis=1, tiled=True),
        lax.all_gather(positive, "grp", axis=1, tiled=True),
    )
    home_set = home_queries[0]
    own_panel = passages[0]
    near_query, near_passage = near_terms(
        home_set, home_targets[0], own_panel, member * panel_rows, logit_scale
    )
    piece_rows = panel_rows // idx_total
    spread = lax.all_to_all(
        own_panel.reshape(idx_total, piece_rows, columns),
        "idx",
        split_axis=0,
        concat_axis=0,
        tiled=True,
    )
    routed = lax.all_to_all(
        jnp.take(spread, partner, axis=0), "idx", split_axis=1, concat_axis=1, tiled=True
    )
    query_acc = near_query
    returned = jnp.zeros((idx_total, piece_rows, columns), jnp.float32)
    for pass_index in range(pass_total):
        query_portion, panel_portion = score_list(
            home_set,
            routed[pass_index].reshape(panel_rows, columns),
            pair_codes[pass_index, own_index, 0],
            pair_count[pass_index, own_index, 0],
            logit_scale,
        )
        query_acc = query_acc + query_portion
        outgoing = panel_portion.astype(jnp.bfloat16).reshape(idx_total, piece_rows, columns)
        arrived = lax.all_to_all(outgoing, "idx", split_axis=0, concat_axis=0, tiled=True)
        returned = returned + jnp.take(arrived, inverse[pass_index], axis=0).astype(jnp.float32)
    far_passage = lax.all_to_all(returned, "idx", split_axis=0, concat_axis=0, tiled=True)
    passage_total = far_passage.reshape(panel_rows, columns) + near_passage
    query_total = lax.psum_scatter(query_acc[None], "grp", scatter_dimension=1, tiled=True)
    return (query_total, passage_total[None])


def dot_nt(a, b):
    return lax.dot_general(a, b, (((1,), (1,)), ((), ())), preferred_element_type=jnp.float32)


def dot_nn(a, b):
    return lax.dot_general(a, b, (((1,), (0,)), ((), ())), preferred_element_type=jnp.float32)


def dot_tn(a, b):
    return lax.dot_general(a, b, (((0,), (0,)), ((), ())), preferred_element_type=jnp.float32)


def fused_kernel(
    n, m, rounds, scale,
    partner_ref, codes_ref, count_ref, q_ref, p_ref, pos_ref,
    qg_ref, pg_ref,
    qall, posall, spread_a, spread_b, stage, routed, grads, arrived, last_a, last_b, fin_out, fin_in,
    part_out, part_in, facc, pacc, wbuf, live, own_panel, local_sem,
    spread_send, spread_recv, q_send, q_recv, pos_send, pos_recv,
    route_send, route_recv, back_send, back_recv, fin_send, fin_recv, part_send, part_recv,
):
    me = lax.axis_index("idx")
    mg = lax.axis_index("grp")
    rows, columns = q_ref.shape
    panel_rows = p_ref.shape[0] * p_ref.shape[1]
    slots = codes_ref.shape[2]
    query_blocks, panel_blocks = m * rows // BLK, panel_rows // BLK
    per_rows = rows // BLK
    piece = p_ref.shape[1]
    spread, last = (spread_a, spread_b), (last_a, last_b)
    chunks = len(spread)
    steps = sorted(range(1, n), key=lambda d: -min(d, n - d))

    def route_parts(r):
        return chunks if r == 0 else 1

    def back_parts(r):
        return chunks if r == rounds - 1 else 1

    def part_rows(h, parts):
        return pl.ds(h * (piece // parts), piece // parts)

    local = [
        pltpu.make_async_copy(q_ref, qall.at[mg], local_sem.at[0]),
        pltpu.make_async_copy(p_ref, own_panel, local_sem.at[1]),
    ] + [
        pltpu.make_async_copy(
            p_ref.at[me, part_rows(h, chunks)], spread[h].at[me], local_sem.at[2 + h]
        )
        for h in range(chunks)
    ]
    for copy in local:
        copy.start()

    barrier = pltpu.get_barrier_semaphore()
    for d in range(1, n):
        pl.semaphore_signal(
            barrier, inc=1, device_id={"idx": lax.rem(me + d, n)}, device_id_type=pl.DeviceIdType.MESH
        )
    for d in range(1, m):
        pl.semaphore_signal(
            barrier, inc=1, device_id={"grp": lax.rem(mg + d, m)}, device_id_type=pl.DeviceIdType.MESH
        )
    pl.semaphore_wait(barrier, n + m - 2)

    def idx_copy(src, dst, send, recv, d):
        return pltpu.make_async_remote_copy(
            src_ref=src, dst_ref=dst, send_sem=send, recv_sem=recv,
            device_id={"idx": lax.rem(me + d, n)}, device_id_type=pl.DeviceIdType.MESH,
        )

    def grp_copy(src, dst, send, recv, d):
        return pltpu.make_async_remote_copy(
            src_ref=src, dst_ref=dst, send_sem=send, recv_sem=recv,
            device_id={"grp": lax.rem(mg + d, m)}, device_id_type=pl.DeviceIdType.MESH,
        )

    def spread_copy(h, d):
        span = part_rows(h, chunks)
        return idx_copy(
            p_ref.at[lax.rem(me + d, n), span], spread[h].at[me],
            spread_send.at[h, d], spread_recv.at[h, d], d,
        )

    def route_copy(r, h, d):
        span = part_rows(h, route_parts(r))
        return idx_copy(
            stage.at[r, lax.rem(me + d, n), span], routed.at[r, me, span],
            route_send.at[r, h, d], route_recv.at[r, h, d], d,
        )

    def back_copy(r, h, d):
        span = part_rows(h, back_parts(r))
        return idx_copy(
            grads.at[r, lax.rem(me + d, n), span],
            last[h].at[me] if r == rounds - 1 else arrived.at[r, me],
            back_send.at[r, h, d], back_recv.at[r, h, d], d,
        )

    def fin_copy(h, d):
        span = part_rows(h, chunks)
        return idx_copy(
            fin_out.at[lax.rem(me + d, n), span], fin_in.at[me, span],
            fin_send.at[h, d], fin_recv.at[h, d], d,
        )

    sibling = mg + 1 - 2 * lax.rem(mg, 2)
    across = lax.rem(mg + 2, m)

    def member_copy(src, dst, send, recv, target):
        return pltpu.make_async_remote_copy(
            src_ref=src, dst_ref=dst, send_sem=send, recv_sem=recv,
            device_id={"grp": target}, device_id_type=pl.DeviceIdType.MESH,
        )

    q_to_across = member_copy(q_ref, qall.at[mg], q_send.at[0], q_recv.at[0], across)
    q_to_sibling = member_copy(q_ref, qall.at[mg], q_send.at[1], q_recv.at[1], sibling)
    q_forward = member_copy(qall.at[across], qall.at[across], q_send.at[2], q_recv.at[2], sibling)

    def pos_copy(d):
        return grp_copy(pos_ref, posall.at[mg], pos_send.at[d], pos_recv.at[d], d)

    def sibling_part(i):
        return member_copy(part_out.at[i], part_in.at[i], part_send.at[i], part_recv.at[i], sibling)

    across_part = member_copy(part_out.at[2], part_in.at[2], part_send.at[2], part_recv.at[2], across)

    for h in range(chunks):
        for d in steps:
            spread_copy(h, d).start()
    for d in range(1, m):
        pos_copy(d).start()
    q_to_across.start()
    q_to_sibling.start()
    posall[mg] = pos_ref[...]

    code_at = panel_blocks * lax.broadcasted_iota(jnp.int32, (query_blocks, panel_rows), 0) + (
        lax.broadcasted_iota(jnp.int32, (query_blocks, panel_rows), 1) // BLK
    )
    for r in range(rounds):
        count = count_ref[r, me]
        hit = jnp.zeros((query_blocks, panel_rows), jnp.float32)
        for k in range(slots):
            code = jnp.where(k < count, codes_ref[r, me, k], -1)
            hit = jnp.where(code_at == code, 1.0, hit)
        for block in range(query_blocks):
            live[r, block // per_rows, block % per_rows] = hit[block : block + 1]

    for copy in local:
        copy.wait()
    for h in range(chunks):
        span = part_rows(h, chunks)
        for d in steps:
            spread_copy(h, d).wait_recv()
        for c in range(n):
            stage[0, c, span] = spread[h][partner_ref[0, c]]
        for d in steps:
            route_copy(0, h, d).start()
    routed[0, me] = stage[0, me]
    q_to_across.wait_recv()
    q_forward.start()
    for r in range(1, rounds):
        for c in range(n):
            for h in range(chunks):
                stage[r, c, part_rows(h, chunks)] = spread[h][partner_ref[r, c]]
        for d in steps:
            for h in range(route_parts(r - 1)):
                route_copy(r - 1, h, d).wait_send()
            route_copy(r, 0, d).start()
        routed[r, me] = stage[r, me]

    for d in range(1, m):
        pos_copy(d).wait_recv()
    q_to_sibling.wait_recv()
    q_forward.wait_recv()

    own = own_panel[...].reshape(panel_rows, columns)
    panel_row = lax.broadcasted_iota(jnp.int32, (panel_rows, rows), 0) + mg * panel_rows
    pg_ref[...] = jnp.zeros(pg_ref.shape, jnp.float32)

    def near_block(h, carry):
        q = qall[h]
        hit = panel_row == posall[h]
        score = scale * jnp.sum(jnp.where(hit, dot_nt(own, q), 0.0), axis=0, keepdims=True)
        coef = positive_weight * (jax.nn.sigmoid(score) - 1.0)
        weight = jnp.where(hit, coef, 0.0)
        high = weight.astype(jnp.bfloat16)
        low = (weight - high.astype(jnp.float32)).astype(jnp.bfloat16)
        pg_ref[...] += dot_nn(high, q) + dot_nn(low, q)
        facc[h] = dot_tn(high, own) + dot_tn(low, own)
        return carry

    for r in range(rounds):
        for h in range(route_parts(r)):
            for d in steps:
                route_copy(r, h, d).wait_recv()
        panel = routed[r].reshape(panel_rows, columns)
        pacc[...] = jnp.zeros(pacc.shape, jnp.float32)

        def score_block(h, carry):
            q = qall[h]
            scores = scale * dot_nt(q, panel)
            mask = jnp.concatenate(
                [jnp.broadcast_to(live[r, h, b], (BLK, panel_rows)) for b in range(per_rows)], axis=0
            )
            weight = jnp.where(mask > 0.0, jax.nn.sigmoid(scores), 0.0).astype(jnp.bfloat16)
            wbuf[h] = weight
            pacc[...] += dot_tn(weight, q)
            return carry

        lax.fori_loop(0, m, score_block, 0)
        grads[r] = (scale * pacc[...]).astype(jnp.bfloat16).reshape(grads.shape[1:])
        for h in range(back_parts(r)):
            for d in steps:
                back_copy(r, h, d).start()
        if r < rounds - 1:
            arrived[r, me] = grads[r, me]
        else:
            for h in range(chunks):
                last[h][me] = grads[r, me, part_rows(h, chunks)]

        if r == 0:
            lax.fori_loop(0, m, near_block, 0)

        if r < rounds - 1:
            def query_block(h, carry):
                facc[h] += dot_nn(wbuf[h], panel)
                return carry

            lax.fori_loop(0, m, query_block, 0)
        else:
            def last_block(i, carry):
                h = lax.rem(sibling + 2 * i, m)
                part_out[i] = (scale * (facc[h] + dot_nn(wbuf[h], panel))).astype(jnp.bfloat16)
                sibling_part(i).start()
                return carry

            lax.fori_loop(0, 2, last_block, 0)
            facc[across] = scale * (facc[across] + dot_nn(wbuf[across], panel))
            sibling_part(1).wait_recv()
            part_out[2] = (facc[across] + part_in[1].astype(jnp.float32)).astype(jnp.bfloat16)
            across_part.start()
            qg_ref[...] = scale * (facc[mg] + dot_nn(wbuf[mg], panel))

    for r in range(rounds - 1):
        for d in steps:
            back_copy(r, 0, d).wait_recv()
    sources = []
    for r in range(rounds):
        for j in range(n):
            source = jnp.int32(0)
            for c in range(n):
                source = jnp.where(partner_ref[r, c] == j, c, source)
            sources.append(source)
    for h in range(chunks):
        span = part_rows(h, chunks)
        for d in steps:
            back_copy(rounds - 1, h, d).wait_recv()
        for j in range(n):
            total = last[h][sources[(rounds - 1) * n + j]].astype(jnp.float32)
            for r in range(rounds - 1):
                total = total + arrived[r, sources[r * n + j], span].astype(jnp.float32)
            fin_out[j, span] = total.astype(jnp.bfloat16)
        for d in steps:
            fin_copy(h, d).start()
    fin_in[me] = fin_out[me]

    sibling_part(0).wait_recv()
    across_part.wait_recv()
    qg_ref[...] += part_in[0].astype(jnp.float32) + part_in[2].astype(jnp.float32)

    for h in range(chunks):
        for d in steps:
            fin_copy(h, d).wait_recv()
    pg_ref[...] = scale * pg_ref[...] + fin_in[...].reshape(panel_rows, columns).astype(jnp.float32)

    for d in steps:
        for h in range(chunks):
            spread_copy(h, d).wait_send()
            fin_copy(h, d).wait_send()
        for h in range(route_parts(rounds - 1)):
            route_copy(rounds - 1, h, d).wait_send()
        for r in range(rounds):
            for h in range(back_parts(r)):
                back_copy(r, h, d).wait_send()
    for d in range(1, m):
        pos_copy(d).wait_send()
    for copy in (q_to_across, q_to_sibling, q_forward, sibling_part(0), sibling_part(1), across_part):
        copy.wait_send()


def fused_shards(queries, passages, partner, pair_codes, pair_count, positive):
    n, m = lax.axis_size("idx"), lax.axis_size("grp")
    rounds = partner.shape[0]
    rows, columns = queries.shape[1:]
    panel_rows = passages.shape[1]
    piece = panel_rows // n
    slots = pair_codes.shape[3]
    bf16, f32, dma = jnp.bfloat16, jnp.float32, pltpu.SemaphoreType.DMA
    vmem, smem = pl.BlockSpec(memory_space=pltpu.VMEM), pl.BlockSpec(memory_space=pltpu.SMEM)
    hbm = pl.BlockSpec(memory_space=pl.ANY)
    pieces, halves = (n, piece, columns), (n, piece // 2, columns)
    query_grad, passage_grad = pl.pallas_call(
        functools.partial(fused_kernel, n, m, rounds, columns ** (-0.5)),
        out_shape=(
            jax.ShapeDtypeStruct((rows, columns), f32),
            jax.ShapeDtypeStruct((panel_rows, columns), f32),
        ),
        in_specs=[smem] * 3 + [hbm] * 2 + [vmem],
        out_specs=(vmem, vmem),
        scratch_shapes=[
            pltpu.VMEM((m, rows, columns), bf16),
            pltpu.VMEM((m, 1, rows), jnp.int32),
            pltpu.VMEM(halves, bf16),
            pltpu.VMEM(halves, bf16),
            pltpu.VMEM((rounds,) + pieces, bf16),
            pltpu.VMEM((rounds,) + pieces, bf16),
            pltpu.VMEM((rounds,) + pieces, bf16),
            pltpu.VMEM((max(rounds - 1, 1),) + pieces, bf16),
            pltpu.VMEM(halves, bf16),
            pltpu.VMEM(halves, bf16),
            pltpu.VMEM(pieces, bf16),
            pltpu.VMEM(pieces, bf16),
            pltpu.VMEM((m, rows, columns), bf16),
            pltpu.VMEM((m, rows, columns), bf16),
            pltpu.VMEM((m, rows, columns), f32),
            pltpu.VMEM((panel_rows, columns), f32),
            pltpu.VMEM((m, rows, panel_rows), bf16),
            pltpu.VMEM((rounds, m, rows // BLK, 1, panel_rows), f32),
            pltpu.VMEM(pieces, bf16),
            dma((4,)),
            dma((2, n)), dma((2, n)), dma((m,)), dma((m,)), dma((m,)), dma((m,)),
            dma((rounds, 2, n)), dma((rounds, 2, n)), dma((rounds, 2, n)), dma((rounds, 2, n)),
            dma((2, n)), dma((2, n)), dma((m,)), dma((m,)),
        ],
        compiler_params=pltpu.CompilerParams(
            collective_id=0, has_side_effects=True, vmem_limit_bytes=56 * 1024 * 1024
        ),
    )(
        partner,
        pair_codes.reshape(rounds, n, slots),
        pair_count.reshape(rounds, n),
        queries[0],
        passages.reshape(pieces),
        positive,
    )
    return (query_grad[None], passage_grad[None])


def shards(queries, passages, partner, pair_codes, pair_count, positive):
    n = lax.axis_size("idx")
    if lax.axis_size("grp") == 4 and passages.shape[1] % (32 * n) == 0 and partner.shape[1] == n:
        return fused_shards(queries, passages, partner, pair_codes, pair_count, positive)
    return plain_shards(queries, passages, partner, pair_codes, pair_count, positive)


def solution(mesh):
    in_specs = (
        P("idx", "grp", None),
        P("idx", "grp", None),
        P(),
        P(None, None, "grp", None),
        P(None, None, "grp"),
        P("idx", "grp"),
    )
    out_specs = (P("idx", "grp", None), P("idx", "grp", None))
    return jax.shard_map(shards, mesh=mesh, in_specs=in_specs, out_specs=out_specs, check_vma=False)
```

```python
import functools
import math

import jax
import jax.numpy as jnp
from jax import lax
from jax.experimental import pallas as pl
from jax.experimental.pallas import tpu as pltpu
from jax.sharding import PartitionSpec as P

BLK = 128


positive_weight = 16.0


def score_list(query_set, panel_shard, pair_list, live_count, logit_scale):
    query_tiles = query_set.shape[0] // BLK
    panel_tiles = panel_shard.shape[0] // BLK
    columns = query_set.shape[1]
    slot_total = pair_list.shape[0]
    group_size = math.gcd(48, slot_total)
    query_grid = query_set.reshape(query_tiles, BLK, columns)
    panel_grid = panel_shard.reshape(panel_tiles, BLK, columns)

    def one_group(turn_index, partial_sums):
        query_acc, panel_acc = partial_sums
        first_slot = turn_index * group_size
        live_mask = first_slot + jnp.arange(group_size, dtype=jnp.int32) < live_count
        query_index = pair_list // panel_tiles
        panel_index = pair_list % panel_tiles
        query_block_list = jnp.take(query_grid, query_index, axis=0)
        panel_block_list = jnp.take(panel_grid, panel_index, axis=0)
        similarity_scores = logit_scale * jnp.einsum(
            "wzr,wlr->wzl", query_block_list, panel_block_list, preferred_element_type=jnp.float32
        )
        sample_weights = jnp.where(
            live_mask[:, None, None], jax.nn.sigmoid(similarity_scores), 0.0
        ).astype(jnp.bfloat16)
        query_portion = jnp.einsum(
            "nku,nua->nka", sample_weights, panel_block_list, preferred_element_type=jnp.float32
        )
        panel_portion = jnp.einsum(
            "swc,swj->scj", sample_weights, query_block_list, preferred_element_type=jnp.float32
        )
        query_acc = query_acc + jax.ops.segment_sum(
            query_portion, query_index, num_segments=query_tiles
        )
        panel_acc = panel_acc + jax.ops.segment_sum(
            panel_portion, panel_index, num_segments=panel_tiles
        )
        return (query_acc, panel_acc)

    start_sums = (
        jnp.zeros(query_grid.shape, jnp.float32),
        jnp.zeros(panel_grid.shape, jnp.float32),
    )
    turn_total = slot_total // group_size
    query_acc, panel_acc = lax.fori_loop(0, turn_total, one_group, start_sums)
    return (
        logit_scale * query_acc.reshape(query_set.shape),
        logit_scale * panel_acc.reshape(panel_shard.shape),
    )


def near_terms(query_set, targets, own_panel, row_offset, logit_scale):
    row_total = own_panel.shape[0]
    local_rows = targets - row_offset
    owned = (local_rows >= 0) & (local_rows < row_total)
    safe_rows = jnp.clip(local_rows, 0, row_total - 1)
    target_rows = jnp.take(own_panel, safe_rows, axis=0).astype(jnp.float32)
    similarity_scores = logit_scale * jnp.sum(query_set.astype(jnp.float32) * target_rows, axis=1)
    factor = jnp.where(owned, positive_weight * (jax.nn.sigmoid(similarity_scores) - 1.0), 0.0)
    query_near = logit_scale * factor[:, None] * target_rows
    panel_near = logit_scale * jax.ops.segment_sum(
        factor[:, None] * query_set.astype(jnp.float32), safe_rows, num_segments=row_total
    )
    return (query_near, panel_near)


def plain_shards(queries, passages, partner, pair_codes, pair_count, positive):
    idx_total = lax.axis_size("idx")
    own_index = lax.axis_index("idx")
    member = lax.axis_index("grp")
    panel_rows = passages.shape[1]
    columns = queries.shape[2]
    pass_total = partner.shape[0]
    logit_scale = columns ** (-0.5)
    inverse = jnp.argsort(partner, axis=1)
    home_queries, home_targets = (
        lax.all_gather(queries, "grp", axis=1, tiled=True),
        lax.all_gather(positive, "grp", axis=1, tiled=True),
    )
    home_set = home_queries[0]
    own_panel = passages[0]
    near_query, near_passage = near_terms(
        home_set, home_targets[0], own_panel, member * panel_rows, logit_scale
    )
    piece_rows = panel_rows // idx_total
    spread = lax.all_to_all(
        own_panel.reshape(idx_total, piece_rows, columns),
        "idx",
        split_axis=0,
        concat_axis=0,
        tiled=True,
    )
    routed = lax.all_to_all(
        jnp.take(spread, partner, axis=0), "idx", split_axis=1, concat_axis=1, tiled=True
    )
    query_acc = near_query
    returned = jnp.zeros((idx_total, piece_rows, columns), jnp.float32)
    for pass_index in range(pass_total):
        query_portion, panel_portion = score_list(
            home_set,
            routed[pass_index].reshape(panel_rows, columns),
            pair_codes[pass_index, own_index, 0],
            pair_count[pass_index, own_index, 0],
            logit_scale,
        )
        query_acc = query_acc + query_portion
        outgoing = panel_portion.astype(jnp.bfloat16).reshape(idx_total, piece_rows, columns)
        arrived = lax.all_to_all(outgoing, "idx", split_axis=0, concat_axis=0, tiled=True)
        returned = returned + jnp.take(arrived, inverse[pass_index], axis=0).astype(jnp.float32)
    far_passage = lax.all_to_all(returned, "idx", split_axis=0, concat_axis=0, tiled=True)
    passage_total = far_passage.reshape(panel_rows, columns) + near_passage
    query_total = lax.psum_scatter(query_acc[None], "grp", scatter_dimension=1, tiled=True)
    return (query_total, passage_total[None])


def dot_nt(a, b):
    return lax.dot_general(a, b, (((1,), (1,)), ((), ())), preferred_element_type=jnp.float32)


def dot_nn(a, b):
    return lax.dot_general(a, b, (((1,), (0,)), ((), ())), preferred_element_type=jnp.float32)


def dot_tn(a, b):
    return lax.dot_general(a, b, (((0,), (0,)), ((), ())), preferred_element_type=jnp.float32)


def fused_kernel(
    n, m, rounds, scale,
    partner_ref, codes_ref, count_ref, q_ref, p_ref, pos_ref,
    qg_ref, pg_ref,
    qall, posall, spread_a, spread_b, stage, routed, grads, arrived, last_a, last_b, fin_out, fin_in,
    part_out, part_in, facc, pacc, wbuf, live, own_panel, local_sem,
    spread_send, spread_recv, q_send, q_recv, pos_send, pos_recv,
    route_send, route_recv, back_send, back_recv, fin_send, fin_recv, part_send, part_recv,
):
    me = lax.axis_index("idx")
    mg = lax.axis_index("grp")
    rows, columns = q_ref.shape
    panel_rows = p_ref.shape[0] * p_ref.shape[1]
    slots = codes_ref.shape[2]
    query_blocks, panel_blocks = m * rows // BLK, panel_rows // BLK
    per_rows = rows // BLK
    piece = p_ref.shape[1]
    spread, last = (spread_a, spread_b), (last_a, last_b)
    chunks = len(spread)
    steps = sorted(range(1, n), key=lambda d: -min(d, n - d))

    def route_parts(r):
        return chunks if r == 0 else 1

    def back_parts(r):
        return chunks if r == rounds - 1 else 1

    def part_rows(h, parts):
        return pl.ds(h * (piece // parts), piece // parts)

    local = [
        pltpu.make_async_copy(q_ref, qall.at[mg], local_sem.at[0]),
        pltpu.make_async_copy(p_ref, own_panel, local_sem.at[1]),
    ] + [
        pltpu.make_async_copy(
            p_ref.at[me, part_rows(h, chunks)], spread[h].at[me], local_sem.at[2 + h]
        )
        for h in range(chunks)
    ]
    for copy in local:
        copy.start()

    barrier = pltpu.get_barrier_semaphore()
    for d in range(1, n):
        pl.semaphore_signal(
            barrier, inc=1, device_id={"idx": lax.rem(me + d, n)}, device_id_type=pl.DeviceIdType.MESH
        )
    for d in range(1, m):
        pl.semaphore_signal(
            barrier, inc=1, device_id={"grp": lax.rem(mg + d, m)}, device_id_type=pl.DeviceIdType.MESH
        )
    pl.semaphore_wait(barrier, n + m - 2)

    def idx_copy(src, dst, send, recv, d):
        return pltpu.make_async_remote_copy(
            src_ref=src, dst_ref=dst, send_sem=send, recv_sem=recv,
            device_id={"idx": lax.rem(me + d, n)}, device_id_type=pl.DeviceIdType.MESH,
        )

    def grp_copy(src, dst, send, recv, d):
        return pltpu.make_async_remote_copy(
            src_ref=src, dst_ref=dst, send_sem=send, recv_sem=recv,
            device_id={"grp": lax.rem(mg + d, m)}, device_id_type=pl.DeviceIdType.MESH,
        )

    def spread_copy(h, d):
        span = part_rows(h, chunks)
        return idx_copy(
            p_ref.at[lax.rem(me + d, n), span], spread[h].at[me],
            spread_send.at[h, d], spread_recv.at[h, d], d,
        )

    def route_copy(r, h, d):
        span = part_rows(h, route_parts(r))
        return idx_copy(
            stage.at[r, lax.rem(me + d, n), span], routed.at[r, me, span],
            route_send.at[r, h, d], route_recv.at[r, h, d], d,
        )

    def back_copy(r, h, d):
        span = part_rows(h, back_parts(r))
        return idx_copy(
            grads.at[r, lax.rem(me + d, n), span],
            last[h].at[me] if r == rounds - 1 else arrived.at[r, me],
            back_send.at[r, h, d], back_recv.at[r, h, d], d,
        )

    def fin_copy(h, d):
        span = part_rows(h, chunks)
        return idx_copy(
            fin_out.at[lax.rem(me + d, n), span], fin_in.at[me, span],
            fin_send.at[h, d], fin_recv.at[h, d], d,
        )

    sibling = mg + 1 - 2 * lax.rem(mg, 2)
    across = lax.rem(mg + 2, m)

    def member_copy(src, dst, send, recv, target):
        return pltpu.make_async_remote_copy(
            src_ref=src, dst_ref=dst, send_sem=send, recv_sem=recv,
            device_id={"grp": target}, device_id_type=pl.DeviceIdType.MESH,
        )

    q_to_across = member_copy(q_ref, qall.at[mg], q_send.at[0], q_recv.at[0], across)
    q_to_sibling = member_copy(q_ref, qall.at[mg], q_send.at[1], q_recv.at[1], sibling)
    q_forward = member_copy(qall.at[across], qall.at[across], q_send.at[2], q_recv.at[2], sibling)

    def pos_copy(d):
        return grp_copy(pos_ref, posall.at[mg], pos_send.at[d], pos_recv.at[d], d)

    def sibling_part(i):
        return member_copy(part_out.at[i], part_in.at[i], part_send.at[i], part_recv.at[i], sibling)

    across_part = member_copy(part_out.at[2], part_in.at[2], part_send.at[2], part_recv.at[2], across)

    for h in range(chunks):
        for d in steps:
            spread_copy(h, d).start()
    for d in range(1, m):
        pos_copy(d).start()
    q_to_across.start()
    q_to_sibling.start()
    posall[mg] = pos_ref[...]

    code_at = panel_blocks * lax.broadcasted_iota(jnp.int32, (query_blocks, panel_rows), 0) + (
        lax.broadcasted_iota(jnp.int32, (query_blocks, panel_rows), 1) // BLK
    )
    for r in range(rounds):
        count = count_ref[r, me]
        hit = jnp.zeros((query_blocks, panel_rows), jnp.float32)
        for k in range(slots):
            code = jnp.where(k < count, codes_ref[r, me, k], -1)
            hit = jnp.where(code_at == code, 1.0, hit)
        for block in range(query_blocks):
            live[r, block // per_rows, block % per_rows] = hit[block : block + 1]

    for copy in local:
        copy.wait()
    for h in range(chunks):
        span = part_rows(h, chunks)
        for d in steps:
            spread_copy(h, d).wait_recv()
        for c in range(n):
            stage[0, c, span] = spread[h][partner_ref[0, c]]
        for d in steps:
            route_copy(0, h, d).start()
    routed[0, me] = stage[0, me]
    q_to_across.wait_recv()
    q_forward.start()
    for r in range(1, rounds):
        for c in range(n):
            for h in range(chunks):
                stage[r, c, part_rows(h, chunks)] = spread[h][partner_ref[r, c]]
        for d in steps:
            route_copy(r, 0, d).start()
        routed[r, me] = stage[r, me]

    for d in range(1, m):
        pos_copy(d).wait_recv()
    q_to_sibling.wait_recv()
    q_forward.wait_recv()

    own = own_panel[...].reshape(panel_rows, columns)
    panel_row = lax.broadcasted_iota(jnp.int32, (panel_rows, rows), 0) + mg * panel_rows
    pg_ref[...] = jnp.zeros(pg_ref.shape, jnp.float32)

    def near_block(h, carry):
        q = qall[h]
        hit = panel_row == posall[h]
        score = scale * jnp.sum(jnp.where(hit, dot_nt(own, q), 0.0), axis=0, keepdims=True)
        coef = positive_weight * (jax.nn.sigmoid(score) - 1.0)
        weight = jnp.where(hit, coef, 0.0)
        high = weight.astype(jnp.bfloat16)
        low = (weight - high.astype(jnp.float32)).astype(jnp.bfloat16)
        pg_ref[...] += dot_nn(high, q) + dot_nn(low, q)
        facc[h] = dot_tn(high, own) + dot_tn(low, own)
        return carry

    for r in range(rounds):
        for h in range(route_parts(r)):
            for d in steps:
                route_copy(r, h, d).wait_recv()
        panel = routed[r].reshape(panel_rows, columns)
        pacc[...] = jnp.zeros(pacc.shape, jnp.float32)

        def score_block(h, carry):
            q = qall[h]
            scores = scale * dot_nt(q, panel)
            mask = jnp.concatenate(
                [jnp.broadcast_to(live[r, h, b], (BLK, panel_rows)) for b in range(per_rows)], axis=0
            )
            weight = jnp.where(mask > 0.0, jax.nn.sigmoid(scores), 0.0).astype(jnp.bfloat16)
            wbuf[h] = weight
            pacc[...] += dot_tn(weight, q)
            return carry

        lax.fori_loop(0, m, score_block, 0)
        grads[r] = (scale * pacc[...]).astype(jnp.bfloat16).reshape(grads.shape[1:])
        for h in range(back_parts(r)):
            for d in steps:
                back_copy(r, h, d).start()
        if r < rounds - 1:
            arrived[r, me] = grads[r, me]
        else:
            for h in range(chunks):
                last[h][me] = grads[r, me, part_rows(h, chunks)]

        if r == 0:
            lax.fori_loop(0, m, near_block, 0)

        if r < rounds - 1:
            def query_block(h, carry):
                facc[h] += dot_nn(wbuf[h], panel)
                return carry

            lax.fori_loop(0, m, query_block, 0)
        else:
            def last_block(i, carry):
                h = lax.rem(sibling + 2 * i, m)
                part_out[i] = (scale * (facc[h] + dot_nn(wbuf[h], panel))).astype(jnp.bfloat16)
                sibling_part(i).start()
                return carry

            lax.fori_loop(0, 2, last_block, 0)
            facc[across] = scale * (facc[across] + dot_nn(wbuf[across], panel))
            sibling_part(1).wait_recv()
            part_out[2] = (facc[across] + part_in[1].astype(jnp.float32)).astype(jnp.bfloat16)
            across_part.start()
            qg_ref[...] = scale * (facc[mg] + dot_nn(wbuf[mg], panel))

    for r in range(rounds - 1):
        for d in steps:
            back_copy(r, 0, d).wait_recv()
    sources = []
    for r in range(rounds):
        for j in range(n):
            source = jnp.int32(0)
            for c in range(n):
                source = jnp.where(partner_ref[r, c] == j, c, source)
            sources.append(source)
    for h in range(chunks):
        span = part_rows(h, chunks)
        for d in steps:
            back_copy(rounds - 1, h, d).wait_recv()
        for j in range(n):
            total = last[h][sources[(rounds - 1) * n + j]].astype(jnp.float32)
            for r in range(rounds - 1):
                total = total + arrived[r, sources[r * n + j], span].astype(jnp.float32)
            fin_out[j, span] = total.astype(jnp.bfloat16)
        for d in steps:
            fin_copy(h, d).start()
    fin_in[me] = fin_out[me]

    sibling_part(0).wait_recv()
    across_part.wait_recv()
    qg_ref[...] += part_in[0].astype(jnp.float32) + part_in[2].astype(jnp.float32)

    for h in range(chunks):
        for d in steps:
            fin_copy(h, d).wait_recv()
    pg_ref[...] = scale * pg_ref[...] + fin_in[...].reshape(panel_rows, columns).astype(jnp.float32)

    for d in steps:
        for h in range(chunks):
            spread_copy(h, d).wait_send()
            fin_copy(h, d).wait_send()
        for r in range(rounds):
            for h in range(route_parts(r)):
                route_copy(r, h, d).wait_send()
            for h in range(back_parts(r)):
                back_copy(r, h, d).wait_send()
    for d in range(1, m):
        pos_copy(d).wait_send()
    for copy in (q_to_across, q_to_sibling, q_forward, sibling_part(0), sibling_part(1), across_part):
        copy.wait_send()


def fused_shards(queries, passages, partner, pair_codes, pair_count, positive):
    n, m = lax.axis_size("idx"), lax.axis_size("grp")
    rounds = partner.shape[0]
    rows, columns = queries.shape[1:]
    panel_rows = passages.shape[1]
    piece = panel_rows // n
    slots = pair_codes.shape[3]
    bf16, f32, dma = jnp.bfloat16, jnp.float32, pltpu.SemaphoreType.DMA
    vmem, smem = pl.BlockSpec(memory_space=pltpu.VMEM), pl.BlockSpec(memory_space=pltpu.SMEM)
    hbm = pl.BlockSpec(memory_space=pl.ANY)
    pieces, halves = (n, piece, columns), (n, piece // 2, columns)
    query_grad, passage_grad = pl.pallas_call(
        functools.partial(fused_kernel, n, m, rounds, columns ** (-0.5)),
        out_shape=(
            jax.ShapeDtypeStruct((rows, columns), f32),
            jax.ShapeDtypeStruct((panel_rows, columns), f32),
        ),
        in_specs=[smem] * 3 + [hbm] * 2 + [vmem],
        out_specs=(vmem, vmem),
        scratch_shapes=[
            pltpu.VMEM((m, rows, columns), bf16),
            pltpu.VMEM((m, 1, rows), jnp.int32),
            pltpu.VMEM(halves, bf16),
            pltpu.VMEM(halves, bf16),
            pltpu.VMEM((rounds,) + pieces, bf16),
            pltpu.VMEM((rounds,) + pieces, bf16),
            pltpu.VMEM((rounds,) + pieces, bf16),
            pltpu.VMEM((max(rounds - 1, 1),) + pieces, bf16),
            pltpu.VMEM(halves, bf16),
            pltpu.VMEM(halves, bf16),
            pltpu.VMEM(pieces, bf16),
            pltpu.VMEM(pieces, bf16),
            pltpu.VMEM((m, rows, columns), bf16),
            pltpu.VMEM((m, rows, columns), bf16),
            pltpu.VMEM((m, rows, columns), f32),
            pltpu.VMEM((panel_rows, columns), f32),
            pltpu.VMEM((m, rows, panel_rows), bf16),
            pltpu.VMEM((rounds, m, rows // BLK, 1, panel_rows), f32),
            pltpu.VMEM(pieces, bf16),
            dma((4,)),
            dma((2, n)), dma((2, n)), dma((m,)), dma((m,)), dma((m,)), dma((m,)),
            dma((rounds, 2, n)), dma((rounds, 2, n)), dma((rounds, 2, n)), dma((rounds, 2, n)),
            dma((2, n)), dma((2, n)), dma((m,)), dma((m,)),
        ],
        compiler_params=pltpu.CompilerParams(
            collective_id=0, has_side_effects=True, vmem_limit_bytes=56 * 1024 * 1024
        ),
    )(
        partner,
        pair_codes.reshape(rounds, n, slots),
        pair_count.reshape(rounds, n),
        queries[0],
        passages.reshape(pieces),
        positive,
    )
    return (query_grad[None], passage_grad[None])


def shards(queries, passages, partner, pair_codes, pair_count, positive):
    n = lax.axis_size("idx")
    if lax.axis_size("grp") == 4 and passages.shape[1] % (32 * n) == 0 and partner.shape[1] == n:
        return fused_shards(queries, passages, partner, pair_codes, pair_count, positive)
    return plain_shards(queries, passages, partner, pair_codes, pair_count, positive)


def solution(mesh):
    in_specs = (
        P("idx", "grp", None),
        P("idx", "grp", None),
        P(),
        P(None, None, "grp", None),
        P(None, None, "grp"),
        P("idx", "grp"),
    )
    out_specs = (P("idx", "grp", None), P("idx", "grp", None))
    return jax.shard_map(shards, mesh=mesh, in_specs=in_specs, out_specs=out_specs, check_vma=False)
```
